32 devices in a mesh: ex: 4 (over z), row: 2 (over core), col: 4 (over y, x).
Axes of the slice: x: 2, y: 2, z: 4, core: 2. Of those that a mesh axis runs over, the one named last changes fastest.
Arguments:
- tokens: bfloat16 [1536, 768], P(('ex', 'row')), may hold values from -6 to 6
- qkv_weight: bfloat16 [768, 2304], P('row', 'col'), may hold values from -0.21875 to 0.21875
- out_weight: bfloat16 [768, 768], P('col', 'row'), may hold values from -1 to 1
- bias_table: float32 [32, 12], P(None, 'col'), may hold values from -4 to 4
- first_norm_scale: float32 [768], replicated, may hold values from 0.5 to 1.5
- second_norm_scale: float32 [768], replicated, may hold values from 0.5 to 1.5
- router_weight: bfloat16 [768, 4], replicated, may hold values from -0.15625 to 0.15625
- expert_in: bfloat16 [4, 768, 3072], P('ex', None, ('row', 'col')), may hold values from -0.21875 to 0.21875
- expert_out: bfloat16 [4, 3072, 768], P('ex', ('row', 'col')), may hold values from -0.4375 to 0.4375
- lengths: int32 [4, 4], P('ex'), may hold values from 1 to 288, 384 in all within a row
- routes: int32 [1536], P(('ex', 'row')), may hold values from 0 to 3, as said below
- slots: int32 [1536], P(('ex', 'row')), may hold values from 0 to 15, as said below
- cotangent: bfloat16 [1536, 768], P(('ex', 'row')), may hold values from -6 to 6
Outputs:
- output: float32 [1536, 768], P(('ex', 'row', 'col'))
- input_grad: float32 [1536, 768], P(('ex', 'row', 'col'))
- qkv_grad: float32 [768, 2304], P('row', 'col')
- out_grad: float32 [768, 768], P('col', 'row')
- table_grad: float32 [32, 12], P(None, 'col')
- norm1_grad: float32 [768], replicated
- norm2_grad: float32 [768], replicated
- router_grad: float32 [768, 4], replicated
- expert_in_grad: float32 [4, 768, 3072], P('ex', None, ('row', 'col'))
- expert_out_grad: float32 [4, 3072, 768], P('ex', ('row', 'col'))
The draws below stay inside these ranges and needn't reach their ends.
Inputs may be any that keep to these rules, and one draw needn't show every extreme that they name: `routes`: in each aligned block of 48 tokens no expert is named by more than 16 tokens, and some expert by exactly 16. `slots`: in each aligned block of 48 tokens no two tokens share both expert and slot. Each group's lengths sum to 384.
All inputs are finite; a program needn't handle non-finite values.
Results may differ from the reference program's by a relative error of at most 0.017.
Values may be sent and summed in bfloat16 or wider, within the bound.
A program may use at most 128 MiB of HBM per device.

```python
import math
import jax
import jax.numpy as jnp
import numpy as np
from jax import lax

D = 768
H = 12
HDIM = 64
FF = 3072
NB = 32
NSEQ = 4
HD = 768
GROUP_TOK = 384
MAXLEN = 288
GROUPS = 4
TOKENS = 1536
DISP = 48
SPECIALIST_TOTAL = 4
CAP = 16


def route_pairs(key):
    blocks = TOKENS // DISP
    pairs = SPECIALIST_TOTAL * CAP
    perturbation_noise_seed, extra_noise_seed, shared_noise_seed, resident_noise_seed, priority_noise_seed = jax.random.split(key, 5)
    gating_perturbation = jax.random.randint(perturbation_noise_seed, (blocks, pairs), 0, 4096)
    extra_preference_values = jax.random.randint(extra_noise_seed, (SPECIALIST_TOTAL,), 0, 3)
    common = jax.random.randint(shared_noise_seed, (), 0, SPECIALIST_TOTAL)
    owned = jax.random.randint(resident_noise_seed, (blocks,), 0, SPECIALIST_TOTAL)
    specialist_choice_index = jnp.arange(pairs, dtype=jnp.int32) // CAP
    gating_probability = gating_perturbation + 1024 * extra_preference_values[specialist_choice_index][None, :]
    gating_probability = gating_probability + 16384 * (specialist_choice_index[None, :] == common).astype(jnp.int32)
    gating_probability = gating_probability + 8192 * (specialist_choice_index[None, :] == owned[:, None]).astype(jnp.int32)
    gating_probability = gating_probability * pairs + jnp.arange(pairs, dtype=jnp.int32)[None, :]
    unused, chosen = lax.top_k(gating_probability, DISP)
    order_scores = jax.random.randint(priority_noise_seed, (blocks, DISP), 0, 32768) * DISP + jnp.arange(DISP, dtype=jnp.int32)[None, :]
    order = jnp.argsort(order_scores, axis=1)
    return jnp.take_along_axis(chosen, order, axis=1).reshape(-1)


def draw_routes(key, part):
    return (route_pairs(key) // CAP).astype(jnp.int32)


def draw_slots(key, part):
    return (route_pairs(key) % CAP).astype(jnp.int32)


def shard_levels(rng, extent, cuts, low, largest):
    def one(axis_at, blocks):
        steps = jax.random.uniform(jax.random.fold_in(jax.random.fold_in(rng, 6), axis_at), (blocks,), jnp.float32, low / len(cuts), largest / len(cuts))
        return jnp.repeat(jnp.exp(steps), extent[axis_at] // blocks).reshape((-1,) + (1,) * (len(extent) - axis_at - 1))

    gain = one(*cuts[0])
    for cut in cuts[1:]:
        gain = gain * one(*cut)
    return gain


def length_profile(count, total, reach, skew):
    loads = [(1 << 20) // math.isqrt(grade ** skew) + 1 for grade in range(2, count + 1)]
    surplus, given = total - reach - (count - 1), [1] * (count - 1)
    while surplus > 0:
        candidates = [i for i in range(count - 1) if given[i] < reach]
        mass, left = sum([loads[i] for i in candidates]), surplus
        for i in candidates:
            extra = min(reach - given[i], max(1, left * loads[i] // mass), surplus)
            given[i] = given[i] + extra
            surplus = surplus - extra
    return np.array([reach] + given)


def ragged(rng, number_of, total, most, skew):
    if number_of == 2:
        one = jax.random.randint(rng, (), max(1, total - most), min(most, total - 1) + 1)
        return jnp.stack([one, total - one])
    sizes = jnp.asarray(length_profile(number_of, total, most, skew), jnp.int32)
    couples = (number_of - 1) // 2
    donor, receiver = sizes[1:1 + 2 * couples:2], sizes[2:2 + 2 * couples:2]
    slack = jnp.minimum(donor - 1, most - receiver)
    passed = jax.random.randint(jax.random.fold_in(rng, 1), (couples,), 0, 1 << 20) % (slack + 1)
    sizes = sizes.at[1:1 + 2 * couples:2].set(donor - passed).at[2:2 + 2 * couples:2].set(receiver + passed)
    return sizes[jax.random.permutation(jax.random.fold_in(rng, 2), number_of)]


def centred(key, shape, width, most, shards=(), kind=jnp.bfloat16):
    entries = jax.random.normal(key, shape, jnp.float32) * width
    if len(shards) > 0:
        entries = shard_levels(key, shape, shards, -0.22, 0.18) * entries
    return jnp.clip(entries, min=-most, max=most).astype(kind)


def setup_inputs(seed: int = 0) -> dict:
    keys = jax.random.split(jax.random.key(seed), 14)
    tokens = centred(keys[0], (TOKENS, D), 1.0, 6.0, ((0, 8),))
    qkv_weight = centred(keys[1], (D, 3 * HD), D ** -0.5, 0.21875, ((0, 2), (1, 4)))
    out_weight = centred(keys[2], (HD, D), (max(1, HD // 24)) ** -0.5, 1.0, ((0, 4), (1, 2)))
    bias_table = centred(keys[3], (NB, H), 1.0, 4.0, ((1, 4),), jnp.float32)
    first_norm_scale = jnp.clip(1.0 + 0.1 * jax.random.normal(keys[4], (D,), jnp.float32), 0.5, 1.5)
    second_norm_scale = jnp.clip(1.0 + 0.1 * jax.random.normal(keys[5], (D,), jnp.float32), 0.5, 1.5)
    router_weight = centred(keys[6], (D, SPECIALIST_TOTAL), (2 * D) ** -0.5, 0.15625)
    expert_in = centred(keys[7], (SPECIALIST_TOTAL, D, FF), D ** -0.5, 0.21875, ((0, 4), (2, 8)))
    expert_out = centred(keys[8], (SPECIALIST_TOTAL, FF, D), (max(1, FF // (SPECIALIST_TOTAL * SPECIALIST_TOTAL))) ** -0.5, 0.4375, ((0, 4), (1, 8)))
    lengths = jax.vmap(lambda own: ragged(own, NSEQ, GROUP_TOK, MAXLEN, 2))(jax.random.split(keys[9], GROUPS)).reshape((GROUPS, NSEQ)).astype(jnp.int32)
    routes = draw_routes(jax.random.fold_in(keys[13], 71), 0)
    slots = draw_slots(jax.random.fold_in(keys[13], 71), 0)
    cotangent = centred(keys[12], (TOKENS, D), 1.0, 6.0, ((0, 8),))
    return dict(tokens=tokens, qkv_weight=qkv_weight, out_weight=out_weight, bias_table=bias_table, first_norm_scale=first_norm_scale, second_norm_scale=second_norm_scale, router_weight=router_weight, expert_in=expert_in, expert_out=expert_out, lengths=lengths, routes=routes, slots=slots, cotangent=cotangent)


EPS = 1e-06
NEG = -1e+30
FAR_STEPS = (12, 16, 23, 32, 46, 64, 91)
HIGH = lax.Precision.HIGHEST

@jax.custom_vjp
def low(v):
    return lax.optimization_barrier(v.astype(jnp.bfloat16)).astype(jnp.float32)

@jax.custom_vjp
def low_back(v):
    return v

def low_keep(v):
    return (low(v), None)

def low_pass(kept, grad):
    return (grad,)

def back_keep(v):
    return (v, None)

def back_low(kept, grad):
    return (low(grad),)
low.defvjp(low_keep, low_pass)
low_back.defvjp(back_keep, back_low)

def bucket_of(rel, buckets):
    dist = jnp.abs(rel)
    far = buckets // 4 + sum(((dist >= step).astype(jnp.int32) for step in FAR_STEPS))
    near = jnp.where(dist < buckets // 4, dist, far)
    return near + buckets // 2 * (rel > 0).astype(jnp.int32)

def forward(tokens, qkv_weight, out_weight, bias_table, first_norm_scale, second_norm_scale, router_weight, expert_in, expert_out, lengths, routes, slots):
    places = jnp.arange(GROUP_TOK, dtype=jnp.int32)
    buckets = bucket_of(places[None, :] - places[:, None], NB)

    def attend_group(item):
        block, sizes = item
        inv = lax.rsqrt(lax.optimization_barrier(jnp.mean(block * block, axis=1, keepdims=True)) + EPS)
        normed = low(block * inv * first_norm_scale)
        qkv = low_back(low(jnp.dot(normed, qkv_weight, precision=HIGH)))
        qkv = qkv.reshape(GROUP_TOK, H, 3, HDIM)
        ends = jnp.cumsum(sizes)
        segment = lax.optimization_barrier(jnp.sum((places[:, None] >= ends[None, :]).astype(jnp.int32), axis=1))
        same = segment[:, None] == segment[None, :]
        bias = jnp.transpose(bias_table[buckets], (2, 0, 1))
        scores = jnp.einsum('qhd,khd->hqk', qkv[:, :, 0], qkv[:, :, 1], precision=HIGH) * HDIM ** (-0.5) + bias
        scores = jnp.where(same[None], low_back(scores), NEG)
        top = lax.optimization_barrier(jnp.max(scores, axis=2, keepdims=True))
        expo = jnp.exp(scores - top)
        prob = low(expo / lax.optimization_barrier(jnp.sum(expo, axis=2, keepdims=True)))
        mixed = jnp.einsum('hqk,khd->qhd', prob, qkv[:, :, 2], precision=HIGH).reshape(GROUP_TOK, H * HDIM)
        mixed = low_back(low(mixed))
        branch = low_back(jnp.dot(mixed, out_weight, precision=HIGH))
        return block + branch
    hidden_state = lax.map(jax.checkpoint(attend_group), (tokens.reshape(GROUPS, GROUP_TOK, D), lengths))
    hidden_state = hidden_state.reshape(TOKENS, D)
    second_inverse_norm = lax.rsqrt(lax.optimization_barrier(jnp.mean(hidden_state * hidden_state, axis=1, keepdims=True)) + EPS)
    normed_two = low(hidden_state * second_inverse_norm * second_norm_scale)
    logits = jnp.dot(normed_two, router_weight, precision=HIGH)
    peak = lax.optimization_barrier(jnp.max(logits, axis=1, keepdims=True))
    raised = jnp.exp(logits - peak)
    gates = raised / lax.optimization_barrier(jnp.sum(raised, axis=1, keepdims=True))
    gate = jnp.take_along_axis(gates, routes[:, None], axis=1)
    blocks = TOKENS // DISP
    index = routes * (blocks * CAP) + jnp.arange(TOKENS, dtype=jnp.int32) // DISP * CAP + slots
    filled = jnp.zeros((SPECIALIST_TOTAL * blocks * CAP, D), jnp.float32).at[index].set(low_back(normed_two))

    def run_expert(item):
        rows, inner, outer = item
        pre = low_back(jnp.dot(rows, inner, precision=HIGH))
        hidden = low(jax.nn.gelu(pre, approximate=True))
        return low_back(low(jnp.dot(hidden, outer, precision=HIGH)))
    produced = lax.map(jax.checkpoint(run_expert), (filled.reshape(SPECIALIST_TOTAL, blocks * CAP, D), expert_in, expert_out))
    returned = produced.reshape(SPECIALIST_TOTAL * blocks * CAP, D)[index]
    return hidden_state + gate * returned

def reference(tokens, qkv_weight, out_weight, bias_table, first_norm_scale, second_norm_scale, router_weight, expert_in, expert_out, lengths, routes, slots, cotangent):
    params = (tokens.astype(jnp.float32), qkv_weight.astype(jnp.float32), out_weight.astype(jnp.float32), bias_table, first_norm_scale, second_norm_scale, router_weight.astype(jnp.float32), expert_in.astype(jnp.float32), expert_out.astype(jnp.float32))

    def wrapped(a, b, c, e, f, g, k, m, n):
        return forward(a, b, c, e, f, g, k, m, n, lengths, routes, slots)
    output, pull = jax.vjp(wrapped, *params)
    grads = pull(cotangent.astype(jnp.float32))
    return (output, grads[0], grads[1], grads[2], grads[3], grads[4], grads[5], grads[6], grads[7], grads[8])
```

```python
import jax
import jax.numpy as jnp
from jax import lax
from jax.experimental import pallas as pl
from jax.experimental.pallas import tpu as pltpu
from jax.sharding import PartitionSpec as P

HDIM = 64


EPS = 1e-06
NEG = -1e30
FAR_STEPS = (12, 16, 23, 32, 46, 64, 91)
HIGH = lax.Precision.HIGHEST
INNER = (((1,), (1,)), ((), ()))
OUTER = (((0,), (0,)), ((), ()))


def bucket_of(rel, buckets):
    dist = jnp.abs(rel)
    far = buckets // 4 + sum(((dist >= step).astype(jnp.int32) for step in FAR_STEPS))
    near = jnp.where(dist < buckets // 4, dist, far)
    return near + buckets // 2 * (rel > 0).astype(jnp.int32)


def toeplitz(vector, rows, cols):
    span = vector.shape[0]
    tiled = jnp.tile(vector, rows)[: rows * (span - 1)]
    return tiled.reshape(rows, span - 1)[:, :cols]


def diagonal_sums(matrix, span):
    rows, cols = matrix.shape
    padded = jnp.pad(matrix, ((0, 0), (0, span - 1 - cols))).reshape(-1)
    padded = jnp.pad(padded, (0, rows))
    return jnp.sum(padded.reshape(rows, span), axis=0)


def gelu_tanh(values):
    return jax.nn.gelu(values, approximate=True)


VMEM = pl.BlockSpec(memory_space=pltpu.VMEM)
DMA = pltpu.SemaphoreType.DMA
VMEM_LIMIT = 48 * 1024 * 1024


def params(collective):
    return pltpu.CompilerParams(
        collective_id=collective, has_side_effects=True, vmem_limit_bytes=VMEM_LIMIT
    )


def remote(src, dst, send, recv, device):
    return pltpu.make_async_remote_copy(
        src_ref=src,
        dst_ref=dst,
        send_sem=send,
        recv_sem=recv,
        device_id=device,
        device_id_type=pl.DeviceIdType.MESH,
    )


def greet(peers):
    barrier = pltpu.get_barrier_semaphore()
    for peer in peers:
        pl.semaphore_signal(
            barrier, inc=1, device_id=peer, device_id_type=pl.DeviceIdType.MESH
        )
    pl.semaphore_wait(barrier, len(peers))


def others(axis):
    size = lax.axis_size(axis)
    me = lax.axis_index(axis)
    return [lax.rem(me + k, size) for k in range(1, size)]


def gather_blocks(block, axis, collective):
    size = lax.axis_size(axis)

    def kernel(x, out, send, recv):
        me = lax.axis_index(axis)
        peers = others(axis)
        greet([{axis: p} for p in peers])
        copies = [
            remote(x, out.at[me], send.at[k], recv.at[k], {axis: p}) for k, p in enumerate(peers)
        ]
        for copy in copies:
            copy.start()
        out[me] = x[...]
        for copy in copies:
            copy.wait()

    return pl.pallas_call(
        kernel,
        out_shape=jax.ShapeDtypeStruct((size, *block.shape), block.dtype),
        in_specs=[VMEM],
        out_specs=VMEM,
        scratch_shapes=[DMA((size - 1,)), DMA((size - 1,))],
        compiler_params=params(collective),
    )(block)


def scatter_sum(blocks, axis, collective):
    size = lax.axis_size(axis)

    def kernel(x, out, land, send, recv):
        me = lax.axis_index(axis)
        peers = others(axis)
        greet([{axis: p} for p in peers])
        copies = [
            remote(x.at[p], land.at[k], send.at[k], recv.at[k], {axis: p})
            for k, p in enumerate(peers)
        ]
        for copy in copies:
            copy.start()
        total = x[me].astype(jnp.float32)
        for k, copy in enumerate(copies):
            copy.wait_recv()
            total = total + land[k].astype(jnp.float32)
        out[...] = total
        for copy in copies:
            copy.wait_send()

    return pl.pallas_call(
        kernel,
        out_shape=jax.ShapeDtypeStruct(blocks.shape[1:], jnp.float32),
        in_specs=[VMEM],
        out_specs=VMEM,
        scratch_shapes=[
            pltpu.VMEM((size - 1, *blocks.shape[1:]), blocks.dtype),
            DMA((size - 1,)),
            DMA((size - 1,)),
        ],
        compiler_params=params(collective),
    )(blocks)


def gather_row(qkv_weight, out_weight, tokens):
    rows, qkv_cols = qkv_weight.shape
    head_rows, half = out_weight.shape
    count, width = tokens.shape

    def kernel(w, o, t, wf, of, tf, send, recv):
        me = lax.axis_index("row")
        peer = {"row": 1 - me}
        greet([peer])
        own_w = wf.at[pl.ds(pl.multiple_of(me * rows, rows), rows)]
        own_o = of.at[:, pl.ds(pl.multiple_of(me * half, half), half)]
        own_t = tf.at[pl.ds(pl.multiple_of(me * count, count), count)]
        copies = [
            remote(t, own_t, send.at[0], recv.at[0], peer),
            remote(w, own_w, send.at[1], recv.at[1], peer),
            remote(o, own_o, send.at[2], recv.at[2], peer),
        ]
        for copy in copies:
            copy.start()
        own_w[...] = w[...]
        own_o[...] = o[...]
        own_t[...] = t[...]
        for copy in copies:
            copy.wait()

    return pl.pallas_call(
        kernel,
        out_shape=(
            jax.ShapeDtypeStruct((2 * rows, qkv_cols), qkv_weight.dtype),
            jax.ShapeDtypeStruct((head_rows, 2 * half), out_weight.dtype),
            jax.ShapeDtypeStruct((2 * count, width), tokens.dtype),
        ),
        in_specs=[VMEM] * 3,
        out_specs=(VMEM,) * 3,
        scratch_shapes=[DMA((3,)), DMA((3,))],
        compiler_params=params(1),
    )(qkv_weight, out_weight, tokens)


def gelu_parts(v):
    root = 0.7978845608028654
    t = jnp.tanh(root * (v + 0.044715 * v * v * v))
    value = 0.5 * v * (1.0 + t)
    slope = 0.5 * (1.0 + t) + 0.5 * v * (1.0 - t * t) * (root * (1.0 + 3 * 0.044715 * v * v))
    return value, slope


def expert_kernel(n_ex, n_col, cap, *refs):
    (out_b, w_in, w_out, back, g_in, g_out, p_in, p_out, land, part, got, summed,
     s_in, s_out, r_in, r_out, wsend, wrecv, xsend, xrecv, csend, crecv,
     psend, precv, bsend, brecv, gsend, grecv) = refs
    bf16, f32 = jnp.bfloat16, jnp.float32
    ex, row, col = lax.axis_index("ex"), lax.axis_index("row"), lax.axis_index("col")
    width = w_in.shape[0]
    tokens = n_ex * n_col * cap
    ex_peers, col_peers = others("ex"), others("col")
    mate = {"row": 1 - row}
    greet([{"ex": p} for p in ex_peers] + [{"col": p} for p in col_peers] + [mate])
    first = [
        remote(out_b.at[p], land.at[col, ex], xsend.at[k], xrecv.at[k], {"ex": p})
        for k, p in enumerate(ex_peers)
    ]
    for copy in first:
        copy.start()
    weights = [
        remote(w_in, p_in, wsend.at[0], wrecv.at[0], mate),
        remote(w_out, p_out, wsend.at[1], wrecv.at[1], mate),
    ]
    land[col, ex] = out_b[ex]
    spread = []

    def forward(slot, index):
        for k, p in enumerate(col_peers):
            copy = remote(
                land.at[col, slot], land.at[col, slot],
                csend.at[index, k], crecv.at[index, k], {"col": p},
            )
            copy.start()
            spread.append(copy)

    forward(ex, 0)
    for copy in weights:
        copy.start()
    for k, copy in enumerate(first):
        copy.wait_recv()
        forward(lax.rem(ex + n_ex - 1 - k, n_ex), 1 + k)
    for copy in spread:
        copy.wait_recv()
    for copy in weights:
        copy.wait()
    x = land[:, :, :cap, :].reshape(tokens, width)
    g = land[:, :, cap:, :].reshape(tokens, width)
    y = jnp.zeros((tokens, width), f32)
    d = jnp.zeros((tokens, width), f32)
    kept = []
    for wi, wo in ((w_in, w_out), (p_in, p_out)):
        pre = jnp.dot(x, wi[...], preferred_element_type=f32)
        value, slope = gelu_parts(pre)
        hid = value.astype(bf16)
        y = y + jnp.dot(hid, wo[...], preferred_element_type=f32)
        d_hid = lax.dot_general(g, wo[...], INNER, preferred_element_type=f32)
        d_pre = (d_hid * slope).astype(bf16)
        d = d + lax.dot_general(d_pre, wi[...], INNER, preferred_element_type=f32)
        kept.append((hid, d_pre))
    part[:, :, :cap, :] = y.astype(bf16).reshape(n_col, n_ex, cap, width)
    part[:, :, cap:, :] = d.astype(bf16).reshape(n_col, n_ex, cap, width)
    sums = [
        remote(part.at[p], got.at[k], psend.at[k], precv.at[k], {"col": p})
        for k, p in enumerate(col_peers)
    ]
    for copy in sums:
        copy.start()
    s_in[...] = lax.dot_general(x, kept[1][1], OUTER, preferred_element_type=f32).astype(bf16)
    s_out[...] = lax.dot_general(kept[1][0], g, OUTER, preferred_element_type=f32).astype(bf16)
    grads = [
        remote(s_in, r_in, gsend.at[0], grecv.at[0], mate),
        remote(s_out, r_out, gsend.at[1], grecv.at[1], mate),
    ]
    for copy in grads:
        copy.start()
    for copy in sums:
        copy.wait_recv()
    total = part[col].astype(f32)
    for k in range(n_col - 1):
        total = total + got[k].astype(f32)
    summed[...] = total.astype(bf16)
    home = [
        remote(summed.at[p], back.at[ex], bsend.at[k], brecv.at[k], {"ex": p})
        for k, p in enumerate(ex_peers)
    ]
    for copy in home:
        copy.start()
    back[ex] = summed[ex]
    g_in[...] = lax.dot_general(x, kept[0][1], OUTER, preferred_element_type=f32)
    g_out[...] = lax.dot_general(kept[0][0], g, OUTER, preferred_element_type=f32)
    for copy in grads:
        copy.wait_recv()
    g_in[...] += r_in[...].astype(f32)
    g_out[...] += r_out[...].astype(f32)
    for copy in home:
        copy.wait()
    for copy in first + spread + sums + grads:
        copy.wait_send()


def expert_block(outbound, w_in, w_out):
    n_ex, twice, width = outbound.shape
    n_col = lax.axis_size("col")
    cap = twice // 2
    bf16 = jnp.bfloat16
    cols = w_in.shape[1]
    return pl.pallas_call(
        lambda *refs: expert_kernel(n_ex, n_col, cap, *refs),
        out_shape=(
            jax.ShapeDtypeStruct((n_ex, twice, width), bf16),
            jax.ShapeDtypeStruct((width, cols), jnp.float32),
            jax.ShapeDtypeStruct((cols, width), jnp.float32),
        ),
        in_specs=[VMEM] * 3,
        out_specs=(VMEM,) * 3,
        scratch_shapes=[
            pltpu.VMEM((width, cols), bf16),
            pltpu.VMEM((cols, width), bf16),
            pltpu.VMEM((n_col, n_ex, twice, width), bf16),
            pltpu.VMEM((n_col, n_ex, twice, width), bf16),
            pltpu.VMEM((n_col - 1, n_ex, twice, width), bf16),
            pltpu.VMEM((n_ex, twice, width), bf16),
            pltpu.VMEM((width, cols), bf16),
            pltpu.VMEM((cols, width), bf16),
            pltpu.VMEM((width, cols), bf16),
            pltpu.VMEM((cols, width), bf16),
            DMA((2,)), DMA((2,)),
            DMA((n_ex - 1,)), DMA((n_ex - 1,)),
            DMA((n_ex, n_col - 1)), DMA((n_ex, n_col - 1)),
            DMA((n_col - 1,)), DMA((n_col - 1,)),
            DMA((n_ex - 1,)), DMA((n_ex - 1,)),
            DMA((2,)), DMA((2,)),
        ],
        compiler_params=params(4),
    )(outbound, w_in, w_out)


def final_kernel(n_ex, *refs):
    (qkv, out, small, qkv_o, out_o, small_o, ql, ol, qs, os_, qx, ox,
     qf, of_, sl, sx, sc, sa, sb,
     rsend, rrecv, esend, erecv, asend, arecv, csend, crecv) = refs
    bf16, f32 = jnp.bfloat16, jnp.float32
    ex, row, col = lax.axis_index("ex"), lax.axis_index("row"), lax.axis_index("col")
    ex_peers, col_peers = others("ex"), others("col")
    mate = {"row": 1 - row}
    greet([{"ex": p} for p in ex_peers] + [{"col": p} for p in col_peers] + [mate])
    waits = []
    one = [
        remote(small, sl, rsend.at[2], rrecv.at[2], mate),
        remote(qkv.at[1 - row], ql, rsend.at[0], rrecv.at[0], mate),
        remote(out.at[1 - row], ol, rsend.at[1], rrecv.at[1], mate),
    ]
    for copy in one:
        copy.start()
    one[0].wait_recv()
    sa[...] = small[...] + sl[...]
    small_ex = [
        remote(sa, sx.at[k], esend.at[2, k], erecv.at[2, k], {"ex": p})
        for k, p in enumerate(ex_peers)
    ]
    for copy in small_ex:
        copy.start()
    one[1].wait_recv()
    qs[...] = (qkv[row].astype(f32) + ql[...].astype(f32)).astype(bf16).reshape(qs.shape)
    q_ex = [
        remote(qs.at[p], qx.at[k], esend.at[0, k], erecv.at[0, k], {"ex": p})
        for k, p in enumerate(ex_peers)
    ]
    for copy in q_ex:
        copy.start()
    one[2].wait_recv()
    os_[...] = (out[row].astype(f32) + ol[...].astype(f32)).astype(bf16).reshape(os_.shape)
    o_ex = [
        remote(os_.at[p], ox.at[k], esend.at[1, k], erecv.at[1, k], {"ex": p})
        for k, p in enumerate(ex_peers)
    ]
    for copy in o_ex:
        copy.start()
    total = sa[...]
    for k, copy in enumerate(small_ex):
        copy.wait_recv()
        total = total + sx[k]
    sb[...] = total
    small_col = [
        remote(sb, sc.at[k], csend.at[k], crecv.at[k], {"col": p})
        for k, p in enumerate(col_peers)
    ]
    for copy in small_col:
        copy.start()
    total = qs[ex].astype(f32)
    for k, copy in enumerate(q_ex):
        copy.wait_recv()
        total = total + qx[k].astype(f32)
    qf[ex] = total.astype(bf16)
    gathers = [
        remote(qf.at[ex], qf.at[ex], asend.at[0, k], arecv.at[0, k], {"ex": p})
        for k, p in enumerate(ex_peers)
    ]
    for copy in gathers:
        copy.start()
    total = os_[ex].astype(f32)
    for k, copy in enumerate(o_ex):
        copy.wait_recv()
        total = total + ox[k].astype(f32)
    of_[ex] = total.astype(bf16)
    more = [
        remote(of_.at[ex], of_.at[ex], asend.at[1, k], arecv.at[1, k], {"ex": p})
        for k, p in enumerate(ex_peers)
    ]
    for copy in more:
        copy.start()
    whole = sb[...]
    for k, copy in enumerate(small_col):
        copy.wait_recv()
        whole = whole + sc[k]
    spot = lax.broadcasted_iota(jnp.int32, whole.shape, 0)
    small_o[...] = jnp.where(spot == 0, sb[...], whole)
    for copy in gathers:
        copy.wait_recv()
    qkv_o[...] = qf[...].astype(f32).reshape(qkv_o.shape)
    for copy in more:
        copy.wait_recv()
    out_o[...] = of_[...].astype(f32).reshape(out_o.shape)
    for copy in one + small_ex + q_ex + o_ex + small_col + gathers + more:
        copy.wait_send()


def final_sums(qkv, out, small):
    n_ex, n_col = lax.axis_size("ex"), lax.axis_size("col")
    bf16, f32 = jnp.bfloat16, jnp.float32
    _, qr, qc = qkv.shape
    _, orr, oc = out.shape
    return pl.pallas_call(
        lambda *refs: final_kernel(n_ex, *refs),
        out_shape=(
            jax.ShapeDtypeStruct((qr, qc), f32),
            jax.ShapeDtypeStruct((orr, oc), f32),
            jax.ShapeDtypeStruct(small.shape, f32),
        ),
        in_specs=[VMEM] * 3,
        out_specs=(VMEM,) * 3,
        scratch_shapes=[
            pltpu.VMEM((qr, qc), bf16),
            pltpu.VMEM((orr, oc), bf16),
            pltpu.VMEM((n_ex, qr // n_ex, qc), bf16),
            pltpu.VMEM((n_ex, orr // n_ex, oc), bf16),
            pltpu.VMEM((n_ex - 1, qr // n_ex, qc), bf16),
            pltpu.VMEM((n_ex - 1, orr // n_ex, oc), bf16),
            pltpu.VMEM((n_ex, qr // n_ex, qc), bf16),
            pltpu.VMEM((n_ex, orr // n_ex, oc), bf16),
            pltpu.VMEM(small.shape, f32),
            pltpu.VMEM((n_ex - 1, *small.shape), f32),
            pltpu.VMEM((n_col - 1, *small.shape), f32),
            pltpu.VMEM(small.shape, f32),
            pltpu.VMEM(small.shape, f32),
            DMA((3,)), DMA((3,)),
            DMA((3, n_ex - 1)), DMA((3, n_ex - 1)),
            DMA((2, n_ex - 1)), DMA((2, n_ex - 1)),
            DMA((n_col - 1,)), DMA((n_col - 1,)),
        ],
        compiler_params=params(8),
    )(qkv, out, small)


def expert_exchange(outbound, w_in, w_out):
    n_ex, twice, width = outbound.shape
    cap = twice // 2
    arrived = lax.all_to_all(outbound, "ex", split_axis=0, concat_axis=0, tiled=True)
    arrived = lax.all_gather(arrived, "col", axis=0, tiled=True)
    x = arrived[:, :cap].reshape(-1, width)
    g = arrived[:, cap:].reshape(-1, width)
    inner = lax.all_gather(w_in, "row", axis=1, tiled=True)
    outer = lax.all_gather(w_out, "row", axis=0, tiled=True)
    pre = jnp.dot(x, inner, preferred_element_type=jnp.float32)
    value, slope = gelu_parts(pre)
    hid = value.astype(jnp.bfloat16)
    y = jnp.dot(hid, outer, preferred_element_type=jnp.float32)
    d_hid = lax.dot_general(g, outer, INNER, preferred_element_type=jnp.float32)
    d_pre = (d_hid * slope).astype(jnp.bfloat16)
    d = lax.dot_general(d_pre, inner, INNER, preferred_element_type=jnp.float32)
    g_in = lax.dot_general(x, d_pre, OUTER, preferred_element_type=jnp.float32)
    g_out = lax.dot_general(hid, g, OUTER, preferred_element_type=jnp.float32)
    both = jnp.concatenate([y.reshape(-1, cap, width), d.reshape(-1, cap, width)], axis=1)
    both = lax.psum_scatter(both, "col", scatter_dimension=0, tiled=True).astype(jnp.bfloat16)
    back = lax.all_to_all(both, "ex", split_axis=0, concat_axis=0, tiled=True)
    g_in = lax.psum_scatter(g_in, "row", scatter_dimension=1, tiled=True)
    g_out = lax.psum_scatter(g_out, "row", scatter_dimension=0, tiled=True)
    return back, g_in, g_out


def on_device(
    tokens,
    qkv_weight,
    out_weight,
    bias_table,
    first_norm_scale,
    second_norm_scale,
    router_weight,
    expert_in,
    expert_out,
    lengths,
    routes,
    slots,
    cotangent,
):
    n_col = lax.axis_size("col")
    my_row = lax.axis_index("row")
    my_col = lax.axis_index("col")
    tokens_per_device, width = tokens.shape
    dispatch_mask = tokens_per_device // n_col
    experts = router_weight.shape[1]
    cap = max(2, (4 * dispatch_mask + 3 * experts - 1) // (3 * experts))
    heads = out_weight.shape[0] // HDIM
    buckets = bias_table.shape[0]
    scale = HDIM ** (-0.5)
    direct = cap % 16 == 0
    qkv_rows, out_rows, group_tokens = gather_row(qkv_weight, out_weight, tokens)
    group = group_tokens.shape[0]
    local_offset = my_row * tokens_per_device
    quarter_offset = my_col * dispatch_mask
    full_sequence = group_tokens.astype(jnp.float32)
    first_inverse_norm = lax.rsqrt(
        jnp.mean(full_sequence * full_sequence, axis=1, keepdims=True) + EPS
    )
    first_unit_input = full_sequence * first_inverse_norm
    first_normed_input = (first_unit_input * first_norm_scale).astype(jnp.bfloat16)
    qkv = jnp.dot(first_normed_input, qkv_rows, preferred_element_type=jnp.float32).astype(
        jnp.bfloat16
    )
    qkv = qkv.reshape(group, heads, 3, HDIM).transpose(2, 1, 0, 3)
    queries = lax.dynamic_slice_in_dim(qkv[0], local_offset, tokens_per_device, 1)
    keys = qkv[1]
    values = qkv[2]
    ends = jnp.cumsum(lengths[0])
    places = jnp.arange(group, dtype=jnp.int32)
    segment = jnp.sum((places[:, None] >= ends[None, :]).astype(jnp.int32), axis=1)
    own_segment = lax.dynamic_slice_in_dim(segment, local_offset, tokens_per_device, 0)
    same = own_segment[:, None] == segment[None, :]
    span = tokens_per_device + group - 1
    offsets = jnp.arange(span, dtype=jnp.int32)
    shifts = jnp.where(offsets < group, offsets, offsets - span) - local_offset
    table_rows = (
        bucket_of(shifts, buckets)[:, None] == jnp.arange(buckets, dtype=jnp.int32)[None, :]
    ).astype(jnp.float32)
    bias_lines = jnp.dot(table_rows, bias_table, precision=HIGH).T

    def scores_of(query, key, line):
        raw = jnp.einsum(
            "qd,kd->qk", query, key, preferred_element_type=jnp.float32
        ) * scale + toeplitz(line, tokens_per_device, group)
        return jnp.where(same, raw, NEG)

    def attend(item):
        query, key, value, line = item
        masked = scores_of(query, key, line)
        top = jnp.max(masked, axis=1, keepdims=True)
        expo = jnp.exp(masked - top)
        total = jnp.sum(expo, axis=1, keepdims=True)
        weights = (expo / total).astype(jnp.bfloat16)
        mixed = jnp.dot(weights, value, preferred_element_type=jnp.float32)
        return (mixed, top + jnp.log(total))

    mixed, log_total = lax.map(attend, (queries, keys, values, bias_lines))
    attn = mixed.transpose(1, 0, 2).reshape(tokens_per_device, heads * HDIM).astype(jnp.bfloat16)
    branch = scatter_sum(
        jnp.dot(attn, out_rows, preferred_element_type=jnp.float32)
        .astype(jnp.bfloat16)
        .reshape(n_col, dispatch_mask, width),
        "col",
        2,
    )
    hidden_state = (
        lax.dynamic_slice_in_dim(tokens, quarter_offset, dispatch_mask, 0).astype(jnp.float32)
        + branch
    )
    second_inverse_norm = lax.rsqrt(
        jnp.mean(hidden_state * hidden_state, axis=1, keepdims=True) + EPS
    )
    second_unit_input = hidden_state * second_inverse_norm
    second_normed_input = (second_unit_input * second_norm_scale).astype(jnp.bfloat16)
    logits = jnp.dot(second_normed_input, router_weight, preferred_element_type=jnp.float32)
    peak = jnp.max(logits, axis=1, keepdims=True)
    raised = jnp.exp(logits - peak)
    gates = raised / jnp.sum(raised, axis=1, keepdims=True)
    route_here = lax.dynamic_slice_in_dim(routes, quarter_offset, dispatch_mask, 0)
    slot_here = lax.dynamic_slice_in_dim(slots, quarter_offset, dispatch_mask, 0)
    picks = (route_here[:, None] == jnp.arange(experts, dtype=jnp.int32)[None, :]).astype(
        jnp.float32
    )
    gate = jnp.sum(gates * picks, axis=1, keepdims=True)
    upstream = lax.dynamic_slice_in_dim(cotangent, quarter_offset, dispatch_mask, 0).astype(
        jnp.float32
    )
    scaled_grad = (gate * upstream).astype(jnp.bfloat16)
    place = route_here * cap + slot_here
    put = (jnp.arange(experts * cap, dtype=jnp.int32)[:, None] == place[None, :]).astype(
        jnp.bfloat16
    )
    outbound = jnp.concatenate(
        [
            jnp.dot(put, rows, preferred_element_type=jnp.float32)
            .astype(jnp.bfloat16)
            .reshape(experts, cap, width)
            for rows in (second_normed_input, scaled_grad)
        ],
        axis=1,
    )
    if direct:
        back, inner_grad, outer_grad = expert_block(outbound, expert_in[0], expert_out[0])
    else:
        back, inner_grad, outer_grad = expert_exchange(outbound, expert_in[0], expert_out[0])
    expert_back_rows, entry_back = (
        lax.dot_general(
            put, rows.reshape(experts * cap, width), OUTER, preferred_element_type=jnp.float32
        )
        for rows in (back[:, :cap], back[:, cap:])
    )
    output = hidden_state + gate * expert_back_rows
    gate_grad = jnp.sum(upstream * expert_back_rows, axis=1, keepdims=True)
    logit_grad = gates * (picks * gate_grad - gate * gate_grad)
    router_part = jnp.dot(second_normed_input.astype(jnp.float32).T, logit_grad, precision=HIGH)
    second_normed_gradient = (
        jnp.dot(logit_grad, router_weight.astype(jnp.float32).T, precision=HIGH) + entry_back
    )
    second_norm_slice = jnp.sum(second_normed_gradient * second_unit_input, axis=0)
    second_scaled_input = second_norm_scale * second_normed_gradient
    state_grad = upstream + second_inverse_norm * (
        second_scaled_input
        - second_unit_input
        * jnp.mean(second_scaled_input * second_unit_input, axis=1, keepdims=True)
    )
    branch_all = gather_blocks(state_grad.astype(jnp.bfloat16), "col", 5).reshape(
        tokens_per_device, width
    )
    out_full = lax.dot_general(attn, branch_all, OUTER, preferred_element_type=jnp.float32)
    attn_grad = lax.dot_general(
        branch_all, out_rows, INNER, preferred_element_type=jnp.float32
    ).astype(jnp.bfloat16)
    attn_grad = attn_grad.reshape(tokens_per_device, heads, HDIM).transpose(1, 0, 2)

    def attend_back(item):
        query, key, value, line, level, grad = item
        masked = scores_of(query, key, line)
        prob = jnp.exp(masked - level)
        weights = prob.astype(jnp.bfloat16)
        prob_grad = jnp.einsum("qd,kd->qk", grad, value, preferred_element_type=jnp.float32)
        value_grad = jnp.einsum("qk,qd->kd", weights, grad, preferred_element_type=jnp.float32)
        score_grad = (prob * (prob_grad - jnp.sum(prob_grad * prob, axis=1, keepdims=True))).astype(
            jnp.bfloat16
        )
        query_grad = jnp.dot(score_grad, key, preferred_element_type=jnp.float32) * scale
        key_grad = (
            jnp.einsum("qk,qd->kd", score_grad, query, preferred_element_type=jnp.float32) * scale
        )
        return (
            query_grad,
            key_grad,
            value_grad,
            diagonal_sums(score_grad.astype(jnp.float32), span),
        )

    query_grads, key_grads, value_grads, diagonals = lax.map(
        attend_back, (queries, keys, values, bias_lines, log_total, attn_grad)
    )
    pairs = jnp.concatenate([key_grads, value_grads], axis=0).astype(jnp.bfloat16)
    pairs = pairs.transpose(1, 0, 2).reshape(2, tokens_per_device, 2 * heads * HDIM)
    own_pairs = scatter_sum(pairs, "row", 6).reshape(tokens_per_device, 2, heads, HDIM)
    key_own, value_own = own_pairs[:, 0], own_pairs[:, 1]
    stacked = jnp.stack(
        [
            query_grads.transpose(1, 0, 2),
            key_own.reshape(tokens_per_device, heads, HDIM),
            value_own.reshape(tokens_per_device, heads, HDIM),
        ],
        axis=2,
    )
    stacked = stacked.reshape(tokens_per_device, 3 * heads * HDIM).astype(jnp.bfloat16)
    xn_own = lax.dynamic_slice_in_dim(first_normed_input, local_offset, tokens_per_device, 0)
    local_unit_input = lax.dynamic_slice_in_dim(
        first_unit_input, local_offset, tokens_per_device, 0
    )
    qkv_full = lax.dot_general(xn_own, stacked, OUTER, preferred_element_type=jnp.float32)
    first_normed_slice = lax.dot_general(
        stacked, qkv_rows, INNER, preferred_element_type=jnp.float32
    )
    first_norm_slice = jnp.sum(first_normed_slice * local_unit_input, axis=0)
    table_part = jnp.dot(table_rows.T, diagonals.T, precision=HIGH)
    xn_one_grad = scatter_sum(
        first_normed_slice.astype(jnp.bfloat16).reshape(n_col, dispatch_mask, width), "col", 7
    )
    quarter_unit_input = lax.dynamic_slice_in_dim(
        local_unit_input, quarter_offset, dispatch_mask, 0
    )
    inv_quarter = lax.dynamic_slice_in_dim(
        first_inverse_norm, local_offset + quarter_offset, dispatch_mask, 0
    )
    first_scaled_input = first_norm_scale * xn_one_grad
    input_grad = state_grad + inv_quarter * (
        first_scaled_input
        - quarter_unit_input
        * jnp.mean(first_scaled_input * quarter_unit_input, axis=1, keepdims=True)
    )
    half = width // lax.axis_size("row")
    if direct:
        flat = jnp.pad(table_part.reshape(1, -1), ((0, 0), (0, width - buckets * heads)))
        small = jnp.concatenate(
            [flat, first_norm_slice[None], second_norm_slice[None], router_part.T], axis=0
        )
        small = jnp.pad(small, ((0, -small.shape[0] % 8), (0, 0)))
        qkv_grad, out_grad, small = final_sums(
            qkv_full.astype(jnp.bfloat16).reshape(2, half, -1),
            out_full.astype(jnp.bfloat16).reshape(-1, 2, half).transpose(1, 0, 2),
            small,
        )
        table_grad = small[0, : buckets * heads].reshape(buckets, heads)
        norm1_grad, norm2_grad, router_grad = small[1], small[2], small[3 : 3 + experts].T
    else:
        qkv_sum, out_sum, table_grad = lax.psum((qkv_full, out_full, table_part), ("ex", "row"))
        norm1_grad, norm2_grad, router_grad = lax.psum(
            (first_norm_slice, second_norm_slice, router_part), ("ex", "row", "col")
        )
        qkv_grad = lax.dynamic_slice_in_dim(qkv_sum, my_row * half, half, 0)
        out_grad = lax.dynamic_slice_in_dim(out_sum, my_row * half, half, 1)
    return (
        output,
        input_grad,
        qkv_grad,
        out_grad,
        table_grad,
        norm1_grad,
        norm2_grad,
        router_grad,
        inner_grad[None],
        outer_grad[None],
    )


def solution(mesh):
    return jax.shard_map(
        on_device,
        mesh=mesh,
        in_specs=(
            P(("ex", "row"), None),
            P("row", "col"),
            P("col", "row"),
            P(None, "col"),
            P(),
            P(),
            P(),
            P("ex", None, ("row", "col")),
            P("ex", ("row", "col"), None),
            P("ex", None),
            P(("ex", "row")),
            P(("ex", "row")),
            P(("ex", "row"), None),
        ),
        out_specs=(
            P(("ex", "row", "col"), None),
            P(("ex", "row", "col"), None),
            P("row", "col"),
            P("col", "row"),
            P(None, "col"),
            P(),
            P(),
            P(),
            P("ex", None, ("row", "col")),
            P("ex", ("row", "col"), None),
        ),
        check_vma=False,
    )
```

```python
import jax
import jax.numpy as jnp
from jax import lax
from jax.experimental import pallas as pl
from jax.experimental.pallas import tpu as pltpu
from jax.sharding import PartitionSpec as P

HDIM = 64


EPS = 1e-06
NEG = -1e30
FAR_STEPS = (12, 16, 23, 32, 46, 64, 91)
HIGH = lax.Precision.HIGHEST
INNER = (((1,), (1,)), ((), ()))
OUTER = (((0,), (0,)), ((), ()))


def bucket_of(rel, buckets):
    dist = jnp.abs(rel)
    far = buckets // 4 + sum(((dist >= step).astype(jnp.int32) for step in FAR_STEPS))
    near = jnp.where(dist < buckets // 4, dist, far)
    return near + buckets // 2 * (rel > 0).astype(jnp.int32)


def toeplitz(vector, rows, cols):
    span = vector.shape[0]
    tiled = jnp.tile(vector, rows)[: rows * (span - 1)]
    return tiled.reshape(rows, span - 1)[:, :cols]


def diagonal_sums(matrix, span):
    rows, cols = matrix.shape
    padded = jnp.pad(matrix, ((0, 0), (0, span - 1 - cols))).reshape(-1)
    padded = jnp.pad(padded, (0, rows))
    return jnp.sum(padded.reshape(rows, span), axis=0)


def gelu_tanh(values):
    return jax.nn.gelu(values, approximate=True)


VMEM = pl.BlockSpec(memory_space=pltpu.VMEM)
DMA = pltpu.SemaphoreType.DMA
VMEM_LIMIT = 48 * 1024 * 1024


def params(collective):
    return pltpu.CompilerParams(
        collective_id=collective, has_side_effects=True, vmem_limit_bytes=VMEM_LIMIT
    )


def remote(src, dst, send, recv, device):
    return pltpu.make_async_remote_copy(
        src_ref=src,
        dst_ref=dst,
        send_sem=send,
        recv_sem=recv,
        device_id=device,
        device_id_type=pl.DeviceIdType.MESH,
    )


def greet(peers):
    barrier = pltpu.get_barrier_semaphore()
    for peer in peers:
        pl.semaphore_signal(
            barrier, inc=1, device_id=peer, device_id_type=pl.DeviceIdType.MESH
        )
    pl.semaphore_wait(barrier, len(peers))


def others(axis):
    size = lax.axis_size(axis)
    me = lax.axis_index(axis)
    return [lax.rem(me + k, size) for k in range(1, size)]


def gather_blocks(block, axis, collective):
    size = lax.axis_size(axis)

    def kernel(x, out, send, recv):
        me = lax.axis_index(axis)
        peers = others(axis)
        greet([{axis: p} for p in peers])
        copies = [
            remote(x, out.at[me], send.at[k], recv.at[k], {axis: p}) for k, p in enumerate(peers)
        ]
        for copy in copies:
            copy.start()
        out[me] = x[...]
        for copy in copies:
            copy.wait()

    return pl.pallas_call(
        kernel,
        out_shape=jax.ShapeDtypeStruct((size, *block.shape), block.dtype),
        in_specs=[VMEM],
        out_specs=VMEM,
        scratch_shapes=[DMA((size - 1,)), DMA((size - 1,))],
        compiler_params=params(collective),
    )(block)


def scatter_sum(blocks, axis, collective):
    size = lax.axis_size(axis)

    def kernel(x, out, land, send, recv):
        me = lax.axis_index(axis)
        peers = others(axis)
        greet([{axis: p} for p in peers])
        copies = [
            remote(x.at[p], land.at[k], send.at[k], recv.at[k], {axis: p})
            for k, p in enumerate(peers)
        ]
        for copy in copies:
            copy.start()
        total = x[me].astype(jnp.float32)
        for k, copy in enumerate(copies):
            copy.wait_recv()
            total = total + land[k].astype(jnp.float32)
        out[...] = total
        for copy in copies:
            copy.wait_send()

    return pl.pallas_call(
        kernel,
        out_shape=jax.ShapeDtypeStruct(blocks.shape[1:], jnp.float32),
        in_specs=[VMEM],
        out_specs=VMEM,
        scratch_shapes=[
            pltpu.VMEM((size - 1, *blocks.shape[1:]), blocks.dtype),
            DMA((size - 1,)),
            DMA((size - 1,)),
        ],
        compiler_params=params(collective),
    )(blocks)


def gather_row(qkv_weight, out_weight, tokens):
    rows, qkv_cols = qkv_weight.shape
    head_rows, half = out_weight.shape
    count, width = tokens.shape

    def kernel(w, o, t, wf, of, tf, send, recv):
        me = lax.axis_index("row")
        peer = {"row": 1 - me}
        greet([peer])
        own_w = wf.at[pl.ds(pl.multiple_of(me * rows, rows), rows)]
        own_o = of.at[:, pl.ds(pl.multiple_of(me * half, half), half)]
        own_t = tf.at[pl.ds(pl.multiple_of(me * count, count), count)]
        copies = [
            remote(t, own_t, send.at[0], recv.at[0], peer),
            remote(w, own_w, send.at[1], recv.at[1], peer),
            remote(o, own_o, send.at[2], recv.at[2], peer),
        ]
        for copy in copies:
            copy.start()
        own_w[...] = w[...]
        own_o[...] = o[...]
        own_t[...] = t[...]
        for copy in copies:
            copy.wait()

    return pl.pallas_call(
        kernel,
        out_shape=(
            jax.ShapeDtypeStruct((2 * rows, qkv_cols), qkv_weight.dtype),
            jax.ShapeDtypeStruct((head_rows, 2 * half), out_weight.dtype),
            jax.ShapeDtypeStruct((2 * count, width), tokens.dtype),
        ),
        in_specs=[VMEM] * 3,
        out_specs=(VMEM,) * 3,
        scratch_shapes=[DMA((3,)), DMA((3,))],
        compiler_params=params(1),
    )(qkv_weight, out_weight, tokens)


def gelu_parts(v):
    root = 0.7978845608028654
    t = jnp.tanh(root * (v + 0.044715 * v * v * v))
    value = 0.5 * v * (1.0 + t)
    slope = 0.5 * (1.0 + t) + 0.5 * v * (1.0 - t * t) * (root * (1.0 + 3 * 0.044715 * v * v))
    return value, slope


def expert_kernel(n_ex, n_col, cap, *refs):
    (out_b, w_in, w_out, back, g_in, g_out, p_in, p_out, land, part, got, summed,
     s_in, s_out, r_in, r_out, wsend, wrecv, xsend, xrecv, csend, crecv,
     psend, precv, bsend, brecv, gsend, grecv) = refs
    bf16, f32 = jnp.bfloat16, jnp.float32
    ex, row, col = lax.axis_index("ex"), lax.axis_index("row"), lax.axis_index("col")
    width = w_in.shape[0]
    tokens = n_ex * n_col * cap
    ex_peers, col_peers = others("ex"), others("col")
    mate = {"row": 1 - row}
    greet([{"ex": p} for p in ex_peers] + [{"col": p} for p in col_peers] + [mate])
    first = [
        remote(out_b.at[p], land.at[col, ex], xsend.at[k], xrecv.at[k], {"ex": p})
        for k, p in enumerate(ex_peers)
    ]
    for copy in first:
        copy.start()
    weights = [
        remote(w_in, p_in, wsend.at[0], wrecv.at[0], mate),
        remote(w_out, p_out, wsend.at[1], wrecv.at[1], mate),
    ]
    land[col, ex] = out_b[ex]
    spread = []

    def forward(slot, index):
        for k, p in enumerate(col_peers):
            copy = remote(
                land.at[col, slot], land.at[col, slot],
                csend.at[index, k], crecv.at[index, k], {"col": p},
            )
            copy.start()
            spread.append(copy)

    forward(ex, 0)
    for copy in weights:
        copy.start()
    for k, copy in enumerate(first):
        copy.wait_recv()
        forward(lax.rem(ex + n_ex - 1 - k, n_ex), 1 + k)
    for copy in spread:
        copy.wait_recv()
    for copy in weights:
        copy.wait()
    x = land[:, :, :cap, :].reshape(tokens, width)
    g = land[:, :, cap:, :].reshape(tokens, width)
    y = jnp.zeros((tokens, width), f32)
    d = jnp.zeros((tokens, width), f32)
    kept = []
    for wi, wo in ((w_in, w_out), (p_in, p_out)):
        pre = jnp.dot(x, wi[...], preferred_element_type=f32)
        value, slope = gelu_parts(pre)
        hid = value.astype(bf16)
        y = y + jnp.dot(hid, wo[...], preferred_element_type=f32)
        d_hid = lax.dot_general(g, wo[...], INNER, preferred_element_type=f32)
        d_pre = (d_hid * slope).astype(bf16)
        d = d + lax.dot_general(d_pre, wi[...], INNER, preferred_element_type=f32)
        kept.append((hid, d_pre))
    part[:, :, :cap, :] = y.astype(bf16).reshape(n_col, n_ex, cap, width)
    part[:, :, cap:, :] = d.astype(bf16).reshape(n_col, n_ex, cap, width)
    sums = [
        remote(part.at[p], got.at[k], psend.at[k], precv.at[k], {"col": p})
        for k, p in enumerate(col_peers)
    ]
    for copy in sums:
        copy.start()
    s_in[...] = lax.dot_general(x, kept[1][1], OUTER, preferred_element_type=f32).astype(bf16)
    s_out[...] = lax.dot_general(kept[1][0], g, OUTER, preferred_element_type=f32).astype(bf16)
    grads = [
        remote(s_in, r_in, gsend.at[0], grecv.at[0], mate),
        remote(s_out, r_out, gsend.at[1], grecv.at[1], mate),
    ]
    for copy in grads:
        copy.start()
    for copy in sums:
        copy.wait_recv()
    total = part[col].astype(f32)
    for k in range(n_col - 1):
        total = total + got[k].astype(f32)
    summed[...] = total.astype(bf16)
    home = [
        remote(summed.at[p], back.at[ex], bsend.at[k], brecv.at[k], {"ex": p})
        for k, p in enumerate(ex_peers)
    ]
    for copy in home:
        copy.start()
    back[ex] = summed[ex]
    g_in[...] = lax.dot_general(x, kept[0][1], OUTER, preferred_element_type=f32)
    g_out[...] = lax.dot_general(kept[0][0], g, OUTER, preferred_element_type=f32)
    for copy in grads:
        copy.wait_recv()
    g_in[...] += r_in[...].astype(f32)
    g_out[...] += r_out[...].astype(f32)
    for copy in home:
        copy.wait()
    for copy in first + spread + sums + grads:
        copy.wait_send()


def expert_block(outbound, w_in, w_out):
    n_ex, twice, width = outbound.shape
    n_col = lax.axis_size("col")
    cap = twice // 2
    bf16 = jnp.bfloat16
    cols = w_in.shape[1]
    return pl.pallas_call(
        lambda *refs: expert_kernel(n_ex, n_col, cap, *refs),
        out_shape=(
            jax.ShapeDtypeStruct((n_ex, twice, width), bf16),
            jax.ShapeDtypeStruct((width, cols), jnp.float32),
            jax.ShapeDtypeStruct((cols, width), jnp.float32),
        ),
        in_specs=[VMEM] * 3,
        out_specs=(VMEM,) * 3,
        scratch_shapes=[
            pltpu.VMEM((width, cols), bf16),
            pltpu.VMEM((cols, width), bf16),
            pltpu.VMEM((n_col, n_ex, twice, width), bf16),
            pltpu.VMEM((n_col, n_ex, twice, width), bf16),
            pltpu.VMEM((n_col - 1, n_ex, twice, width), bf16),
            pltpu.VMEM((n_ex, twice, width), bf16),
            pltpu.VMEM((width, cols), bf16),
            pltpu.VMEM((cols, width), bf16),
            pltpu.VMEM((width, cols), bf16),
            pltpu.VMEM((cols, width), bf16),
            DMA((2,)), DMA((2,)),
            DMA((n_ex - 1,)), DMA((n_ex - 1,)),
            DMA((n_ex, n_col - 1)), DMA((n_ex, n_col - 1)),
            DMA((n_col - 1,)), DMA((n_col - 1,)),
            DMA((n_ex - 1,)), DMA((n_ex - 1,)),
            DMA((2,)), DMA((2,)),
        ],
        compiler_params=params(4),
    )(outbound, w_in, w_out)


def bias_of(line, rows, cols):
    return pltpu.roll(
        jnp.broadcast_to(line, (rows, line.shape[1])), 0, 1, stride=1, stride_axis=0
    )[:, :cols]


def diagonals_of(matrix, span):
    rows, cols = matrix.shape
    wide = jnp.concatenate([matrix, jnp.zeros((rows, span - cols), matrix.dtype)], axis=1)
    acc = wide[:8]
    for tile in range(1, rows // 8):
        acc = acc + pltpu.roll(wide[8 * tile : 8 * tile + 8], span - 8 * tile, 1)
    line = acc[:1]
    for row in range(1, 8):
        line = line + pltpu.roll(acc[row : row + 1], span - row, 1)
    return line


def back_kernel(n_ex, n_col, heads, *refs):
    (sg, sgf, attn, outw, q, k, v, level, lines, seg_q, seg_k, xn, unit, qkvw, small, rows_t,
     unit_q, inv_q, gain, input_o, qkv_o, out_o, small_o,
     ba, prob_s, kvb, kvl, st, tb, tl, qs, qx, qf, ob, ol, os_, ox, of_, xb, xl,
     sa, sl, sx, sb, sc,
     bs, br, ks, kr, ts, tr, qss, qsr, qas, qar, os1, or1, os2, or2, os3, or3,
     xs, xr, ss1, sr1, ss2, sr2, ss3, sr3) = refs
    bf16, f32 = jnp.bfloat16, jnp.float32
    ex, row, col = lax.axis_index("ex"), lax.axis_index("row"), lax.axis_index("col")
    ex_peers, col_peers = others("ex"), others("col")
    mate = {"row": 1 - row}
    greet([{"col": p} for p in col_peers] + [{"ex": p} for p in ex_peers] + [mate])
    everything = []

    def go(copies):
        for copy in copies:
            copy.start()
        everything.extend(copies)
        return copies

    first = go(
        [remote(sg, ba.at[col], bs.at[i], br.at[i], {"col": p}) for i, p in enumerate(col_peers)]
    )
    ba[col] = sg[...]
    count, width = xn.shape
    group = k.shape[1]
    span = lines.shape[2]
    half = width // 2
    scale = HDIM ** (-0.5)
    same = seg_q[...] == seg_k[...]
    for h in range(heads):
        raw = lax.dot_general(q[h], k[h], INNER, preferred_element_type=f32)
        raw = raw * scale + bias_of(lines[h], count, group)
        prob_s[h] = jnp.exp(jnp.where(same, raw, NEG) - level[h])
    for copy in first:
        copy.wait_recv()
    branch = ba[...].reshape(count, width)
    d_attn = lax.dot_general(branch, outw[...], INNER, preferred_element_type=f32).astype(bf16)
    out_full = lax.dot_general(attn[...], branch, OUTER, preferred_element_type=f32).astype(bf16)
    ob[0] = out_full[:, :half]
    ob[1] = out_full[:, half:]
    out_one = go([remote(ob.at[1 - row], ol, os1.at[0], or1.at[0], mate)])

    d_query, diags, kv_copies, t_copies, q_copies, a_copies = {}, [], {}, {}, {}, {}

    def head(h):
        prob = prob_s[h]
        g = d_attn[:, h * HDIM : (h + 1) * HDIM]
        d_prob = lax.dot_general(g, v[h], INNER, preferred_element_type=f32)
        mean = jnp.sum(d_prob * prob, axis=1, keepdims=True)
        ds = (prob * (d_prob - mean)).astype(bf16)
        d_key = lax.dot_general(ds, q[h], OUTER, preferred_element_type=f32) * scale
        d_val = lax.dot_general(prob.astype(bf16), g, OUTER, preferred_element_type=f32)
        kvb[h] = (
            jnp.concatenate([d_key, d_val], axis=1).astype(bf16).reshape(2, count, 2 * HDIM)
        )
        kv_copies[h] = go([remote(kvb.at[h, 1 - row], kvl.at[h], ks.at[h], kr.at[h], mate)])
        d_query[h] = jnp.dot(ds, k[h], preferred_element_type=f32) * scale
        diags.append(diagonals_of(ds.astype(f32), span))

    def finish(h):
        kv_copies[h][0].wait_recv()
        pair = kvb[h, row].astype(f32) + kvl[h].astype(f32)
        rows = jnp.concatenate([d_query[h], pair], axis=1).astype(bf16)
        st[h] = rows
        full = lax.dot_general(rows, xn[...], OUTER, preferred_element_type=f32).astype(bf16)
        tb[h, 0] = full[:, :half]
        tb[h, 1] = full[:, half:]
        t_copies[h] = go([remote(tb.at[h, 1 - row], tl.at[h], ts.at[h], tr.at[h], mate)])

    def second(h):
        t_copies[h][0].wait_recv()
        both = tb[h, row].astype(f32) + tl[h].astype(f32)
        qs[h] = both.astype(bf16).reshape(qs.shape[1:])
        q_copies[h] = go(
            [
                remote(qs.at[h, p], qx.at[h, i], qss.at[h, i], qsr.at[h, i], {"ex": p})
                for i, p in enumerate(ex_peers)
            ]
        )

    def third(h):
        total = qs[h, ex].astype(f32)
        for i, copy in enumerate(q_copies[h]):
            copy.wait_recv()
            total = total + qx[h, i].astype(f32)
        qf[h, ex] = total.astype(bf16)
        a_copies[h] = go(
            [
                remote(qf.at[h, ex], qf.at[h, ex], qas.at[h, i], qar.at[h, i], {"ex": p})
                for i, p in enumerate(ex_peers)
            ]
        )

    head(0)
    for h in range(1, heads):
        head(h)
        if h >= 2:
            second(h - 2)
        finish(h - 1)
        if h == 1:
            out_one[0].wait_recv()
            both = ob[row].astype(f32) + ol[...].astype(f32)
            os_[...] = both.astype(bf16).reshape(os_.shape)
            out_two = go(
                [
                    remote(os_.at[p], ox.at[i], os2.at[i], or2.at[i], {"ex": p})
                    for i, p in enumerate(ex_peers)
                ]
            )
    finish(heads - 1)
    second(heads - 2)
    rows = jnp.concatenate([st[h] for h in range(heads)], axis=1)
    d_xn = lax.dot_general(rows, qkvw[...], INNER, preferred_element_type=f32)
    xb[...] = d_xn.astype(bf16).reshape(xb.shape)
    x_copies = go(
        [remote(xb.at[p], xl.at[i], xs.at[i], xr.at[i], {"col": p}) for i, p in enumerate(col_peers)]
    )
    second(heads - 1)
    norm = jnp.sum(d_xn * unit[...], axis=0, keepdims=True)
    diag = jnp.concatenate(diags + [jnp.zeros((8 - heads, span), f32)], axis=0)
    table = jnp.dot(diag, rows_t[...], precision=HIGH, preferred_element_type=f32)
    spot = lax.broadcasted_iota(jnp.int32, small.shape, 0)
    sa[:, :width] = jnp.where(spot == 0, norm, small[...])
    sa[:, width:] = table
    small_one = go([remote(sa, sl, ss1.at[0], sr1.at[0], mate)])
    third(0)
    small_one[0].wait_recv()
    sb[0] = sa[...] + sl[...]
    small_two = go(
        [
            remote(sb.at[0], sx.at[i], ss2.at[i], sr2.at[i], {"ex": p})
            for i, p in enumerate(ex_peers)
        ]
    )
    total = os_[ex].astype(f32)
    for i, copy in enumerate(out_two):
        copy.wait_recv()
        total = total + ox[i].astype(f32)
    of_[ex] = total.astype(bf16)
    out_three = go(
        [
            remote(of_.at[ex], of_.at[ex], os3.at[i], or3.at[i], {"ex": p})
            for i, p in enumerate(ex_peers)
        ]
    )
    third(1)
    d_own = xb[col].astype(f32)
    for i, copy in enumerate(x_copies):
        copy.wait_recv()
        d_own = d_own + xl[i].astype(f32)
    scaled = gain[...] * d_own
    inner = jnp.sum(scaled * unit_q[...], axis=1, keepdims=True) * (1.0 / width)
    input_o[...] = sgf[...] + inv_q[...] * (scaled - unit_q[...] * inner)
    for h in range(2, heads):
        third(h)
    total = sb[0]
    for i, copy in enumerate(small_two):
        copy.wait_recv()
        total = total + sx[i]
    sb[1] = total
    small_three = go(
        [
            remote(sb.at[1], sc.at[i], ss3.at[i], sr3.at[i], {"col": p})
            for i, p in enumerate(col_peers)
        ]
    )
    for copy in out_three:
        copy.wait_recv()
    out_o[...] = of_[...].astype(f32).reshape(out_o.shape)
    for i, copy in enumerate(small_three):
        copy.wait_recv()
        total = total + sc[i]
    small_o[:, :width] = total[:, :width]
    small_o[:, width:] = sb[1, :, width:]
    for h in range(heads):
        for copy in a_copies[h]:
            copy.wait_recv()
        piece = qf[h].astype(f32).reshape(3 * HDIM, half)
        qkv_o[:, h * 3 * HDIM : (h + 1) * 3 * HDIM] = piece.T
    for copy in everything:
        copy.wait_send()


def back_block(sg, sgf, attn, outw, q, k, v, level, lines, seg_q, seg_k, xn, unit, qkvw, small,
               rows_t, unit_q, inv_q, gain):
    n_ex, n_col = lax.axis_size("ex"), lax.axis_size("col")
    bf16, f32 = jnp.bfloat16, jnp.float32
    heads, group, _ = k.shape
    count, width = xn.shape
    quarter = sg.shape[0]
    half = width // 2
    tri = 3 * HDIM
    wide = width + rows_t.shape[1]
    head_rows = outw.shape[0]
    args = (sg, sgf, attn, outw, q, k, v, level, lines, seg_q, seg_k, xn, unit, qkvw, small,
            rows_t, unit_q, inv_q, gain)
    V = pltpu.VMEM
    return pl.pallas_call(
        lambda *refs: back_kernel(n_ex, n_col, heads, *refs),
        out_shape=(
            jax.ShapeDtypeStruct((quarter, width), f32),
            jax.ShapeDtypeStruct((half, heads * tri), f32),
            jax.ShapeDtypeStruct((head_rows, half), f32),
            jax.ShapeDtypeStruct((8, wide), f32),
        ),
        in_specs=[VMEM] * len(args),
        out_specs=(VMEM,) * 4,
        scratch_shapes=[
            V((n_col, quarter, width), bf16),
            V((heads, count, group), f32),
            V((heads, 2, count, 2 * HDIM), bf16),
            V((heads, count, 2 * HDIM), bf16),
            V((heads, count, tri), bf16),
            V((heads, 2, tri, half), bf16),
            V((heads, tri, half), bf16),
            V((heads, n_ex, tri // n_ex, half), bf16),
            V((heads, n_ex - 1, tri // n_ex, half), bf16),
            V((heads, n_ex, tri // n_ex, half), bf16),
            V((2, head_rows, half), bf16),
            V((head_rows, half), bf16),
            V((n_ex, head_rows // n_ex, half), bf16),
            V((n_ex - 1, head_rows // n_ex, half), bf16),
            V((n_ex, head_rows // n_ex, half), bf16),
            V((n_col, quarter, width), bf16),
            V((n_col - 1, quarter, width), bf16),
            V((8, wide), f32),
            V((8, wide), f32),
            V((n_ex - 1, 8, wide), f32),
            V((2, 8, wide), f32),
            V((n_col - 1, 8, wide), f32),
            DMA((n_col - 1,)), DMA((n_col - 1,)),
            DMA((heads,)), DMA((heads,)),
            DMA((heads,)), DMA((heads,)),
            DMA((heads, n_ex - 1)), DMA((heads, n_ex - 1)),
            DMA((heads, n_ex - 1)), DMA((heads, n_ex - 1)),
            DMA((1,)), DMA((1,)),
            DMA((n_ex - 1,)), DMA((n_ex - 1,)),
            DMA((n_ex - 1,)), DMA((n_ex - 1,)),
            DMA((n_col - 1,)), DMA((n_col - 1,)),
            DMA((1,)), DMA((1,)),
            DMA((n_ex - 1,)), DMA((n_ex - 1,)),
            DMA((n_col - 1,)), DMA((n_col - 1,)),
        ],
        compiler_params=params(8),
    )(*args)


def expert_exchange(outbound, w_in, w_out):
    n_ex, twice, width = outbound.shape
    cap = twice // 2
    arrived = lax.all_to_all(outbound, "ex", split_axis=0, concat_axis=0, tiled=True)
    arrived = lax.all_gather(arrived, "col", axis=0, tiled=True)
    x = arrived[:, :cap].reshape(-1, width)
    g = arrived[:, cap:].reshape(-1, width)
    inner = lax.all_gather(w_in, "row", axis=1, tiled=True)
    outer = lax.all_gather(w_out, "row", axis=0, tiled=True)
    pre = jnp.dot(x, inner, preferred_element_type=jnp.float32)
    value, slope = gelu_parts(pre)
    hid = value.astype(jnp.bfloat16)
    y = jnp.dot(hid, outer, preferred_element_type=jnp.float32)
    d_hid = lax.dot_general(g, outer, INNER, preferred_element_type=jnp.float32)
    d_pre = (d_hid * slope).astype(jnp.bfloat16)
    d = lax.dot_general(d_pre, inner, INNER, preferred_element_type=jnp.float32)
    g_in = lax.dot_general(x, d_pre, OUTER, preferred_element_type=jnp.float32)
    g_out = lax.dot_general(hid, g, OUTER, preferred_element_type=jnp.float32)
    both = jnp.concatenate([y.reshape(-1, cap, width), d.reshape(-1, cap, width)], axis=1)
    both = lax.psum_scatter(both, "col", scatter_dimension=0, tiled=True).astype(jnp.bfloat16)
    back = lax.all_to_all(both, "ex", split_axis=0, concat_axis=0, tiled=True)
    g_in = lax.psum_scatter(g_in, "row", scatter_dimension=1, tiled=True)
    g_out = lax.psum_scatter(g_out, "row", scatter_dimension=0, tiled=True)
    return back, g_in, g_out


def on_device(
    tokens,
    qkv_weight,
    out_weight,
    bias_table,
    first_norm_scale,
    second_norm_scale,
    router_weight,
    expert_in,
    expert_out,
    lengths,
    routes,
    slots,
    cotangent,
):
    n_col = lax.axis_size("col")
    my_row = lax.axis_index("row")
    my_col = lax.axis_index("col")
    tokens_per_device, width = tokens.shape
    dispatch_mask = tokens_per_device // n_col
    experts = router_weight.shape[1]
    cap = max(2, (4 * dispatch_mask + 3 * experts - 1) // (3 * experts))
    heads = out_weight.shape[0] // HDIM
    buckets = bias_table.shape[0]
    scale = HDIM ** (-0.5)
    direct = cap % 16 == 0
    qkv_rows, out_rows, group_tokens = gather_row(qkv_weight, out_weight, tokens)
    group = group_tokens.shape[0]
    local_offset = my_row * tokens_per_device
    quarter_offset = my_col * dispatch_mask
    full_sequence = group_tokens.astype(jnp.float32)
    first_inverse_norm = lax.rsqrt(
        jnp.mean(full_sequence * full_sequence, axis=1, keepdims=True) + EPS
    )
    first_unit_input = full_sequence * first_inverse_norm
    first_normed_input = (first_unit_input * first_norm_scale).astype(jnp.bfloat16)
    qkv = jnp.dot(first_normed_input, qkv_rows, preferred_element_type=jnp.float32).astype(
        jnp.bfloat16
    )
    qkv = qkv.reshape(group, heads, 3, HDIM).transpose(2, 1, 0, 3)
    queries = lax.dynamic_slice_in_dim(qkv[0], local_offset, tokens_per_device, 1)
    keys = qkv[1]
    values = qkv[2]
    ends = jnp.cumsum(lengths[0])
    places = jnp.arange(group, dtype=jnp.int32)
    segment = jnp.sum((places[:, None] >= ends[None, :]).astype(jnp.int32), axis=1)
    own_segment = lax.dynamic_slice_in_dim(segment, local_offset, tokens_per_device, 0)
    same = own_segment[:, None] == segment[None, :]
    span = -(-(tokens_per_device + group - 1) // 128) * 128
    offsets = jnp.arange(span, dtype=jnp.int32)
    shifts = jnp.where(offsets < group, offsets, offsets - span) - local_offset
    table_rows = (
        bucket_of(shifts, buckets)[:, None] == jnp.arange(buckets, dtype=jnp.int32)[None, :]
    ).astype(jnp.float32)
    bias_lines = jnp.dot(table_rows, bias_table, precision=HIGH).T

    def scores_of(query, key, line):
        raw = jnp.einsum(
            "qd,kd->qk", query, key, preferred_element_type=jnp.float32
        ) * scale + toeplitz(line, tokens_per_device, group)
        return jnp.where(same, raw, NEG)

    def attend(item):
        query, key, value, line = item
        masked = scores_of(query, key, line)
        top = jnp.max(masked, axis=1, keepdims=True)
        expo = jnp.exp(masked - top)
        total = jnp.sum(expo, axis=1, keepdims=True)
        weights = (expo / total).astype(jnp.bfloat16)
        mixed = jnp.dot(weights, value, preferred_element_type=jnp.float32)
        return (mixed, top + jnp.log(total))

    mixed, log_total = lax.map(attend, (queries, keys, values, bias_lines))
    attn = mixed.transpose(1, 0, 2).reshape(tokens_per_device, heads * HDIM).astype(jnp.bfloat16)
    branch = scatter_sum(
        jnp.dot(attn, out_rows, preferred_element_type=jnp.float32)
        .astype(jnp.bfloat16)
        .reshape(n_col, dispatch_mask, width),
        "col",
        2,
    )
    hidden_state = (
        lax.dynamic_slice_in_dim(tokens, quarter_offset, dispatch_mask, 0).astype(jnp.float32)
        + branch
    )
    second_inverse_norm = lax.rsqrt(
        jnp.mean(hidden_state * hidden_state, axis=1, keepdims=True) + EPS
    )
    second_unit_input = hidden_state * second_inverse_norm
    second_normed_input = (second_unit_input * second_norm_scale).astype(jnp.bfloat16)
    logits = jnp.dot(second_normed_input, router_weight, preferred_element_type=jnp.float32)
    peak = jnp.max(logits, axis=1, keepdims=True)
    raised = jnp.exp(logits - peak)
    gates = raised / jnp.sum(raised, axis=1, keepdims=True)
    route_here = lax.dynamic_slice_in_dim(routes, quarter_offset, dispatch_mask, 0)
    slot_here = lax.dynamic_slice_in_dim(slots, quarter_offset, dispatch_mask, 0)
    picks = (route_here[:, None] == jnp.arange(experts, dtype=jnp.int32)[None, :]).astype(
        jnp.float32
    )
    gate = jnp.sum(gates * picks, axis=1, keepdims=True)
    upstream = lax.dynamic_slice_in_dim(cotangent, quarter_offset, dispatch_mask, 0).astype(
        jnp.float32
    )
    scaled_grad = (gate * upstream).astype(jnp.bfloat16)
    place = route_here * cap + slot_here
    put = (jnp.arange(experts * cap, dtype=jnp.int32)[:, None] == place[None, :]).astype(
        jnp.bfloat16
    )
    outbound = jnp.concatenate(
        [
            jnp.dot(put, rows, preferred_element_type=jnp.float32)
            .astype(jnp.bfloat16)
            .reshape(experts, cap, width)
            for rows in (second_normed_input, scaled_grad)
        ],
        axis=1,
    )
    if direct:
        back, inner_grad, outer_grad = expert_block(outbound, expert_in[0], expert_out[0])
    else:
        back, inner_grad, outer_grad = expert_exchange(outbound, expert_in[0], expert_out[0])
    expert_back_rows, entry_back = (
        lax.dot_general(
            put, rows.reshape(experts * cap, width), OUTER, preferred_element_type=jnp.float32
        )
        for rows in (back[:, :cap], back[:, cap:])
    )
    output = hidden_state + gate * expert_back_rows
    gate_grad = jnp.sum(upstream * expert_back_rows, axis=1, keepdims=True)
    logit_grad = gates * (picks * gate_grad - gate * gate_grad)
    router_part = jnp.dot(second_normed_input.astype(jnp.float32).T, logit_grad, precision=HIGH)
    second_normed_gradient = (
        jnp.dot(logit_grad, router_weight.astype(jnp.float32).T, precision=HIGH) + entry_back
    )
    second_norm_slice = jnp.sum(second_normed_gradient * second_unit_input, axis=0)
    second_scaled_input = second_norm_scale * second_normed_gradient
    state_grad = upstream + second_inverse_norm * (
        second_scaled_input
        - second_unit_input
        * jnp.mean(second_scaled_input * second_unit_input, axis=1, keepdims=True)
    )
    xn_own = lax.dynamic_slice_in_dim(first_normed_input, local_offset, tokens_per_device, 0)
    local_unit_input = lax.dynamic_slice_in_dim(
        first_unit_input, local_offset, tokens_per_device, 0
    )
    quarter_unit_input = lax.dynamic_slice_in_dim(
        local_unit_input, quarter_offset, dispatch_mask, 0
    )
    inv_quarter = lax.dynamic_slice_in_dim(
        first_inverse_norm, local_offset + quarter_offset, dispatch_mask, 0
    )
    if direct:
        small = jnp.concatenate(
            [jnp.zeros((1, width), jnp.float32), second_norm_slice[None], router_part.T], axis=0
        )
        small = jnp.pad(small, ((0, 8 - small.shape[0]), (0, 0)))
        input_grad, qkv_grad, out_grad, small = back_block(
            state_grad.astype(jnp.bfloat16),
            state_grad,
            attn,
            out_rows,
            queries,
            keys,
            values,
            log_total,
            bias_lines[:, None, :],
            own_segment[:, None],
            segment[None, :],
            xn_own,
            local_unit_input,
            qkv_rows,
            small,
            jnp.pad(table_rows, ((0, 0), (0, 128 - buckets))),
            quarter_unit_input,
            inv_quarter,
            first_norm_scale[None, :],
        )
        norm1_grad, norm2_grad = small[0, :width], small[1, :width]
        router_grad = small[2 : 2 + experts, :width].T
        table_grad = small[:heads, width : width + buckets].T
        return (
            output,
            input_grad,
            qkv_grad,
            out_grad,
            table_grad,
            norm1_grad,
            norm2_grad,
            router_grad,
            inner_grad[None],
            outer_grad[None],
        )
    branch_all = gather_blocks(state_grad.astype(jnp.bfloat16), "col", 5).reshape(
        tokens_per_device, width
    )
    out_full = lax.dot_general(attn, branch_all, OUTER, preferred_element_type=jnp.float32)
    attn_grad = lax.dot_general(
        branch_all, out_rows, INNER, preferred_element_type=jnp.float32
    ).astype(jnp.bfloat16)
    attn_grad = attn_grad.reshape(tokens_per_device, heads, HDIM).transpose(1, 0, 2)

    def attend_back(item):
        query, key, value, line, level, grad = item
        masked = scores_of(query, key, line)
        prob = jnp.exp(masked - level)
        weights = prob.astype(jnp.bfloat16)
        prob_grad = jnp.einsum("qd,kd->qk", grad, value, preferred_element_type=jnp.float32)
        value_grad = jnp.einsum("qk,qd->kd", weights, grad, preferred_element_type=jnp.float32)
        score_grad = (prob * (prob_grad - jnp.sum(prob_grad * prob, axis=1, keepdims=True))).astype(
            jnp.bfloat16
        )
        query_grad = jnp.dot(score_grad, key, preferred_element_type=jnp.float32) * scale
        key_grad = (
            jnp.einsum("qk,qd->kd", score_grad, query, preferred_element_type=jnp.float32) * scale
        )
        return (
            query_grad,
            key_grad,
            value_grad,
            diagonal_sums(score_grad.astype(jnp.float32), span),
        )

    query_grads, key_grads, value_grads, diagonals = lax.map(
        attend_back, (queries, keys, values, bias_lines, log_total, attn_grad)
    )
    pairs = jnp.concatenate([key_grads, value_grads], axis=0).astype(jnp.bfloat16)
    pairs = pairs.transpose(1, 0, 2).reshape(2, tokens_per_device, 2 * heads * HDIM)
    own_pairs = scatter_sum(pairs, "row", 6).reshape(tokens_per_device, 2, heads, HDIM)
    key_own, value_own = own_pairs[:, 0], own_pairs[:, 1]
    stacked = jnp.stack(
        [
            query_grads.transpose(1, 0, 2),
            key_own.reshape(tokens_per_device, heads, HDIM),
            value_own.reshape(tokens_per_device, heads, HDIM),
        ],
        axis=2,
    )
    stacked = stacked.reshape(tokens_per_device, 3 * heads * HDIM).astype(jnp.bfloat16)
    qkv_full = lax.dot_general(xn_own, stacked, OUTER, preferred_element_type=jnp.float32)
    first_normed_slice = lax.dot_general(
        stacked, qkv_rows, INNER, preferred_element_type=jnp.float32
    )
    first_norm_slice = jnp.sum(first_normed_slice * local_unit_input, axis=0)
    table_part = jnp.dot(table_rows.T, diagonals.T, precision=HIGH)
    xn_one_grad = scatter_sum(
        first_normed_slice.astype(jnp.bfloat16).reshape(n_col, dispatch_mask, width), "col", 7
    )
    first_scaled_input = first_norm_scale * xn_one_grad
    input_grad = state_grad + inv_quarter * (
        first_scaled_input
        - quarter_unit_input
        * jnp.mean(first_scaled_input * quarter_unit_input, axis=1, keepdims=True)
    )
    half = width // lax.axis_size("row")
    qkv_sum, out_sum, table_grad = lax.psum((qkv_full, out_full, table_part), ("ex", "row"))
    norm1_grad, norm2_grad, router_grad = lax.psum(
        (first_norm_slice, second_norm_slice, router_part), ("ex", "row", "col")
    )
    qkv_grad = lax.dynamic_slice_in_dim(qkv_sum, my_row * half, half, 0)
    out_grad = lax.dynamic_slice_in_dim(out_sum, my_row * half, half, 1)
    return (
        output,
        input_grad,
        qkv_grad,
        out_grad,
        table_grad,
        norm1_grad,
        norm2_grad,
        router_grad,
        inner_grad[None],
        outer_grad[None],
    )


def solution(mesh):
    return jax.shard_map(
        on_device,
        mesh=mesh,
        in_specs=(
            P(("ex", "row"), None),
            P("row", "col"),
            P("col", "row"),
            P(None, "col"),
            P(),
            P(),
            P(),
            P("ex", None, ("row", "col")),
            P("ex", ("row", "col"), None),
            P("ex", None),
            P(("ex", "row")),
            P(("ex", "row")),
            P(("ex", "row"), None),
        ),
        out_specs=(
            P(("ex", "row", "col"), None),
            P(("ex", "row", "col"), None),
            P("row", "col"),
            P("col", "row"),
            P(None, "col"),
            P(),
            P(),
            P(),
            P("ex", None, ("row", "col")),
            P("ex", ("row", "col"), None),
        ),
        check_vma=False,
    )
```

```python
import jax
import jax.numpy as jnp
from jax import lax
from jax.experimental import pallas as pl
from jax.experimental.pallas import tpu as pltpu
from jax.sharding import PartitionSpec as P

HDIM = 64


EPS = 1e-06
NEG = -1e30
FAR_STEPS = (12, 16, 23, 32, 46, 64, 91)
HIGH = lax.Precision.HIGHEST
INNER = (((1,), (1,)), ((), ()))
OUTER = (((0,), (0,)), ((), ()))


def bucket_of(rel, buckets):
    dist = jnp.abs(rel)
    far = buckets // 4 + sum(((dist >= step).astype(jnp.int32) for step in FAR_STEPS))
    near = jnp.where(dist < buckets // 4, dist, far)
    return near + buckets // 2 * (rel > 0).astype(jnp.int32)


def toeplitz(vector, rows, cols):
    span = vector.shape[0]
    tiled = jnp.tile(vector, rows)[: rows * (span - 1)]
    return tiled.reshape(rows, span - 1)[:, :cols]


def diagonal_sums(matrix, span):
    rows, cols = matrix.shape
    padded = jnp.pad(matrix, ((0, 0), (0, span - 1 - cols))).reshape(-1)
    padded = jnp.pad(padded, (0, rows))
    return jnp.sum(padded.reshape(rows, span), axis=0)


def gelu_tanh(values):
    return jax.nn.gelu(values, approximate=True)


VMEM = pl.BlockSpec(memory_space=pltpu.VMEM)
DMA = pltpu.SemaphoreType.DMA
VMEM_LIMIT = 48 * 1024 * 1024


def params(collective):
    return pltpu.CompilerParams(
        collective_id=collective, has_side_effects=True, vmem_limit_bytes=VMEM_LIMIT
    )


def remote(src, dst, send, recv, device):
    return pltpu.make_async_remote_copy(
        src_ref=src,
        dst_ref=dst,
        send_sem=send,
        recv_sem=recv,
        device_id=device,
        device_id_type=pl.DeviceIdType.MESH,
    )


def greet(peers):
    barrier = pltpu.get_barrier_semaphore()
    for peer in peers:
        pl.semaphore_signal(
            barrier, inc=1, device_id=peer, device_id_type=pl.DeviceIdType.MESH
        )
    pl.semaphore_wait(barrier, len(peers))


def others(axis):
    size = lax.axis_size(axis)
    me = lax.axis_index(axis)
    return [lax.rem(me + k, size) for k in range(1, size)]


def gather_blocks(block, axis, collective):
    size = lax.axis_size(axis)

    def kernel(x, out, send, recv):
        me = lax.axis_index(axis)
        peers = others(axis)
        greet([{axis: p} for p in peers])
        copies = [
            remote(x, out.at[me], send.at[k], recv.at[k], {axis: p}) for k, p in enumerate(peers)
        ]
        for copy in copies:
            copy.start()
        out[me] = x[...]
        for copy in copies:
            copy.wait()

    return pl.pallas_call(
        kernel,
        out_shape=jax.ShapeDtypeStruct((size, *block.shape), block.dtype),
        in_specs=[VMEM],
        out_specs=VMEM,
        scratch_shapes=[DMA((size - 1,)), DMA((size - 1,))],
        compiler_params=params(collective),
    )(block)


def scatter_sum(blocks, axis, collective):
    size = lax.axis_size(axis)

    def kernel(x, out, land, send, recv):
        me = lax.axis_index(axis)
        peers = others(axis)
        greet([{axis: p} for p in peers])
        copies = [
            remote(x.at[p], land.at[k], send.at[k], recv.at[k], {axis: p})
            for k, p in enumerate(peers)
        ]
        for copy in copies:
            copy.start()
        total = x[me].astype(jnp.float32)
        for k, copy in enumerate(copies):
            copy.wait_recv()
            total = total + land[k].astype(jnp.float32)
        out[...] = total
        for copy in copies:
            copy.wait_send()

    return pl.pallas_call(
        kernel,
        out_shape=jax.ShapeDtypeStruct(blocks.shape[1:], jnp.float32),
        in_specs=[VMEM],
        out_specs=VMEM,
        scratch_shapes=[
            pltpu.VMEM((size - 1, *blocks.shape[1:]), blocks.dtype),
            DMA((size - 1,)),
            DMA((size - 1,)),
        ],
        compiler_params=params(collective),
    )(blocks)


def gather_row(qkv_weight, out_weight, tokens):
    rows, qkv_cols = qkv_weight.shape
    head_rows, half = out_weight.shape
    count, width = tokens.shape

    def kernel(w, o, t, wf, of, tf, send, recv):
        me = lax.axis_index("row")
        peer = {"row": 1 - me}
        greet([peer])
        own_w = wf.at[pl.ds(pl.multiple_of(me * rows, rows), rows)]
        own_o = of.at[:, pl.ds(pl.multiple_of(me * half, half), half)]
        own_t = tf.at[pl.ds(pl.multiple_of(me * count, count), count)]
        copies = [
            remote(t, own_t, send.at[0], recv.at[0], peer),
            remote(w, own_w, send.at[1], recv.at[1], peer),
            remote(o, own_o, send.at[2], recv.at[2], peer),
        ]
        for copy in copies:
            copy.start()
        own_w[...] = w[...]
        own_o[...] = o[...]
        own_t[...] = t[...]
        for copy in copies:
            copy.wait()

    return pl.pallas_call(
        kernel,
        out_shape=(
            jax.ShapeDtypeStruct((2 * rows, qkv_cols), qkv_weight.dtype),
            jax.ShapeDtypeStruct((head_rows, 2 * half), out_weight.dtype),
            jax.ShapeDtypeStruct((2 * count, width), tokens.dtype),
        ),
        in_specs=[VMEM] * 3,
        out_specs=(VMEM,) * 3,
        scratch_shapes=[DMA((3,)), DMA((3,))],
        compiler_params=params(1),
    )(qkv_weight, out_weight, tokens)


def gelu_parts(v):
    root = 0.7978845608028654
    t = jnp.tanh(root * (v + 0.044715 * v * v * v))
    value = 0.5 * v * (1.0 + t)
    slope = 0.5 * (1.0 + t) + 0.5 * v * (1.0 - t * t) * (root * (1.0 + 3 * 0.044715 * v * v))
    return value, slope


def bias_of(line, rows, cols):
    return pltpu.roll(
        jnp.broadcast_to(line, (rows, line.shape[1])), 0, 1, stride=1, stride_axis=0
    )[:, :cols]


def diagonals_of(matrix, span):
    rows, cols = matrix.shape
    wide = jnp.concatenate([matrix, jnp.zeros((rows, span - cols), matrix.dtype)], axis=1)
    acc = wide[:8]
    for tile in range(1, rows // 8):
        acc = acc + pltpu.roll(wide[8 * tile : 8 * tile + 8], span - 8 * tile, 1)
    line = acc[:1]
    for row in range(1, 8):
        line = line + pltpu.roll(acc[row : row + 1], span - row, 1)
    return line


def whole_kernel(dims, names, *refs):
    n_ex, n_col, heads, cap, buckets, count, width, quarter = dims
    r = dict(zip(names, refs))
    bf16, f32 = jnp.bfloat16, jnp.float32
    ex, row, col = lax.axis_index("ex"), lax.axis_index("row"), lax.axis_index("col")
    ex_peers, col_peers = others("ex"), others("col")
    mate = {"row": 1 - row}
    group = 2 * count
    half = width // 2
    tri = 3 * HDIM
    span = -(-(count + group - 1) // 128) * 128
    scale = HDIM ** (-0.5)
    slots = n_ex * cap
    everything = []

    def go(pairs):
        copies = []
        for source, target, device in pairs:
            at = len(everything)
            copy = remote(source, target, r["send"].at[at], r["recv"].at[at], device)
            copy.start()
            everything.append(copy)
            copies.append(copy)
        return copies

    def dot(a, b, how=(((1,), (0,)), ((), ())), precision=None):
        return lax.dot_general(a, b, how, precision=precision, preferred_element_type=f32)

    greet([mate] + [{"col": p} for p in col_peers] + [{"ex": p} for p in ex_peers])
    tokens, qkv_w, out_w = r["tokens"], r["qkv_weight"], r["out_weight"]
    w_in, w_out = r["expert_in"], r["expert_out"]
    tf, qkvw, outw = r["tf"], r["qkvw"], r["outw"]
    own_t = tf.at[pl.ds(pl.multiple_of(row * count, count), count)]
    own_w = qkvw.at[pl.ds(pl.multiple_of(row * half, half), half)]
    own_o = outw.at[:, pl.ds(pl.multiple_of(row * half, half), half)]
    entry = go([(tokens, own_t, mate), (qkv_w, own_w, mate), (out_w, own_o, mate)])
    weights = go([(w_in.at[0], r["p_in"], mate), (w_out.at[0], r["p_out"], mate)])
    own_t[...] = tokens[...]
    own_w[...] = qkv_w[...]
    own_o[...] = out_w[...]
    gain1, gain2 = r["gain1"][...], r["gain2"][...]

    place = lax.broadcasted_iota(jnp.int32, (span, 128), 0)
    shift = jnp.where(place < group, place, place - span) - row * count
    rows_t = (
        bucket_of(shift, buckets) == lax.broadcasted_iota(jnp.int32, (span, 128), 1)
    ).astype(f32)
    r["rows_t"][...] = rows_t
    lines = dot(r["table"][...], rows_t, INNER, HIGH)
    lengths = r["lengths"][...]
    own = lax.broadcasted_iota(jnp.int32, (count, 1), 0) + row * count
    all_keys = lax.broadcasted_iota(jnp.int32, (1, group), 1)
    seg_q = jnp.zeros((count, 1), jnp.int32)
    seg_k = jnp.zeros((1, group), jnp.int32)
    end = jnp.zeros((1, 1), jnp.int32)
    for s in range(lengths.shape[1]):
        end = end + lengths[:, s : s + 1]
        seg_q = seg_q + (own >= end).astype(jnp.int32)
        seg_k = seg_k + (all_keys >= end).astype(jnp.int32)
    same = seg_q == seg_k

    def normed(block):
        wide = block.astype(f32)
        inverse = lax.rsqrt(jnp.mean(wide * wide, axis=1, keepdims=True) + EPS)
        return wide * inverse, inverse

    entry[0].wait_recv()
    r["xn"][...] = (normed(tf[...])[0] * gain1).astype(bf16)
    entry[1].wait_recv()
    r["qkv"][...] = dot(r["xn"][...], qkvw[...]).astype(bf16)
    mine = r["qkv"][pl.ds(pl.multiple_of(row * count, count), count), :]
    mixed = []
    for h in range(heads):
        at = h * tri
        r["q"][h] = mine[:, at : at + HDIM]
        r["k"][h] = r["qkv"][:, at + HDIM : at + 2 * HDIM]
        r["v"][h] = r["qkv"][:, at + 2 * HDIM : at + 3 * HDIM]
        raw = dot(r["q"][h], r["k"][h], INNER)
        raw = raw * scale + bias_of(lines[h : h + 1], count, group)
        raw = jnp.where(same, raw, NEG)
        expo = jnp.exp(raw - jnp.max(raw, axis=1, keepdims=True))
        prob = expo / jnp.sum(expo, axis=1, keepdims=True)
        r["prob"][h] = prob
        mixed.append(dot(prob.astype(bf16), r["v"][h]))
    r["attn"][...] = jnp.concatenate(mixed, axis=1).astype(bf16)
    entry[2].wait_recv()
    r["bb"][...] = dot(r["attn"][...], outw[...]).astype(bf16).reshape(n_col, quarter, width)
    copies = go([(r["bb"].at[p], r["bl"].at[i], {"col": p}) for i, p in enumerate(col_peers)])
    here = pl.ds(pl.multiple_of(col * quarter, quarter), quarter)
    put = (
        lax.broadcasted_iota(jnp.int32, (slots, quarter), 0) == r["place"][col]
    ).astype(f32)
    owner = lax.broadcasted_iota(jnp.int32, (slots, n_ex), 0)
    kind = lax.broadcasted_iota(jnp.int32, (slots, n_ex), 1) * cap
    owner = ((owner >= kind) & (owner < kind + cap)).astype(f32)
    picks = dot(put, owner, OUTER)
    put = put.astype(bf16)
    upstream = r["cotangent"][here, :].astype(f32)
    state = tokens[here, :].astype(f32) + r["bb"][col].astype(f32)
    for i, copy in enumerate(copies):
        copy.wait_recv()
        state = state + r["bl"][i].astype(f32)
    unit2, inv2 = normed(state)
    xn2 = (unit2 * gain2).astype(bf16)
    logits = dot(xn2, r["router"][...])
    raised = jnp.exp(logits - jnp.max(logits, axis=1, keepdims=True))
    gates = raised / jnp.sum(raised, axis=1, keepdims=True)
    gate = jnp.sum(gates * picks, axis=1, keepdims=True)
    outb = r["outb"]
    outb[:, :cap, :] = dot(put, xn2).astype(bf16).reshape(n_ex, cap, width)
    scaled = (gate * upstream).astype(bf16)
    outb[:, cap:, :] = dot(put, scaled).astype(bf16).reshape(n_ex, cap, width)

    land = r["land"]
    first = go([(outb.at[p], land.at[col, ex], {"ex": p}) for p in ex_peers])
    land[col, ex] = outb[ex]
    spread = go([(land.at[col, ex], land.at[col, ex], {"col": p}) for p in col_peers])
    for i, copy in enumerate(first):
        copy.wait_recv()
        slot = lax.rem(ex + n_ex - 1 - i, n_ex)
        spread += go([(land.at[col, slot], land.at[col, slot], {"col": p}) for p in col_peers])
    for copy in weights + spread:
        copy.wait_recv()
    many = n_col * n_ex * cap
    x = land[:, :, :cap, :].reshape(many, width)
    g = land[:, :, cap:, :].reshape(many, width)
    y = jnp.zeros((many, width), f32)
    d = jnp.zeros((many, width), f32)
    kept = []
    for wi, wo in ((w_in[0], w_out[0]), (r["p_in"][...], r["p_out"][...])):
        value, slope = gelu_parts(dot(x, wi))
        hid = value.astype(bf16)
        y = y + dot(hid, wo)
        d_pre = (dot(g, wo, INNER) * slope).astype(bf16)
        d = d + dot(d_pre, wi, INNER)
        kept.append((hid, d_pre))
    part = r["part"]
    part[:, :, :cap, :] = y.astype(bf16).reshape(n_col, n_ex, cap, width)
    part[:, :, cap:, :] = d.astype(bf16).reshape(n_col, n_ex, cap, width)
    sums = go([(part.at[p], r["got"].at[i], {"col": p}) for i, p in enumerate(col_peers)])
    r["s_in"][...] = dot(x, kept[1][1], OUTER).astype(bf16)
    r["s_out"][...] = dot(kept[1][0], g, OUTER).astype(bf16)
    grads = go([(r["s_in"], r["r_in"], mate), (r["s_out"], r["r_out"], mate)])
    r["g_in"][0] = dot(x, kept[0][1], OUTER)
    r["g_out"][0] = dot(kept[0][0], g, OUTER)
    total = part[col].astype(f32)
    for i, copy in enumerate(sums):
        copy.wait_recv()
        total = total + r["got"][i].astype(f32)
    r["summed"][...] = total.astype(bf16)
    back = r["back"]
    home = go([(r["summed"].at[p], back.at[ex], {"ex": p}) for p in ex_peers])
    back[ex] = r["summed"][ex]
    unit, inv1 = normed(tokens[...])
    r["unit"][...] = unit
    for copy in home:
        copy.wait_recv()

    expert_y = dot(put, back[:, :cap, :].reshape(slots, width), OUTER)
    d_entry = dot(put, back[:, cap:, :].reshape(slots, width), OUTER)
    r["output"][...] = state + gate * expert_y
    d_gate = jnp.sum(upstream * expert_y, axis=1, keepdims=True)
    d_logits = gates * (picks * d_gate - gate * d_gate)
    d_xn2 = dot(d_logits, r["router"][...].astype(f32), INNER, HIGH) + d_entry
    u2 = gain2 * d_xn2
    d_state = upstream + inv2 * (u2 - unit2 * jnp.mean(u2 * unit2, axis=1, keepdims=True))
    r["ds"][...] = d_state
    ba = r["ba"]
    ba[col] = d_state.astype(bf16)
    copies = go([(ba.at[col], ba.at[col], {"col": p}) for p in col_peers])
    sa = r["sa"]
    sa[...] = jnp.zeros(sa.shape, f32)
    sa[1:2, :width] = jnp.sum(d_xn2 * unit2, axis=0, keepdims=True)
    sa[2 : 2 + n_ex, :width] = dot(d_logits, xn2.astype(f32), OUTER, HIGH)
    for copy in grads:
        copy.wait_recv()
    r["g_in"][0] += r["r_in"][...].astype(f32)
    r["g_out"][0] += r["r_out"][...].astype(f32)
    for copy in copies:
        copy.wait_recv()
    branch = ba[...].reshape(count, width)
    d_attn = dot(branch, outw[...], INNER).astype(bf16)
    kvb, kvl, st, tb, tl = r["kvb"], r["kvl"], r["st"], r["tb"], r["tl"]
    qs, qx, qf = r["qs"], r["qx"], r["qf"]
    ob, ol, os_, ox, of_ = r["ob"], r["ol"], r["os"], r["ox"], r["of"]
    own_xn = r["xn"][pl.ds(pl.multiple_of(row * count, count), count), :]
    d_query, diags, kv_copies, t_copies, q_copies, a_copies = {}, [], {}, {}, {}, {}

    def head(h):
        prob = r["prob"][h]
        grad = d_attn[:, h * HDIM : (h + 1) * HDIM]
        d_prob = dot(grad, r["v"][h], INNER)
        mean = jnp.sum(d_prob * prob, axis=1, keepdims=True)
        ds = (prob * (d_prob - mean)).astype(bf16)
        d_key = dot(ds, r["q"][h], OUTER) * scale
        d_val = dot(prob.astype(bf16), grad, OUTER)
        kvb[h] = (
            jnp.concatenate([d_key, d_val], axis=1).astype(bf16).reshape(2, count, 2 * HDIM)
        )
        kv_copies[h] = go([(kvb.at[h, 1 - row], kvl.at[h], mate)])
        d_query[h] = dot(ds, r["k"][h]) * scale
        r["dsc"][h] = ds

    def finish(h):
        kv_copies[h][0].wait_recv()
        pair = kvb[h, row].astype(f32) + kvl[h].astype(f32)
        rows = jnp.concatenate([d_query[h], pair], axis=1).astype(bf16)
        st[h] = rows
        full = dot(rows, own_xn, OUTER).astype(bf16)
        tb[h, 0] = full[:, :half]
        tb[h, 1] = full[:, half:]
        t_copies[h] = go([(tb.at[h, 1 - row], tl.at[h], mate)])

    def second(h):
        t_copies[h][0].wait_recv()
        both = tb[h, row].astype(f32) + tl[h].astype(f32)
        qs[h] = both.astype(bf16).reshape(qs.shape[1:])
        q_copies[h] = go(
            [(qs.at[h, p], qx.at[h, i], {"ex": p}) for i, p in enumerate(ex_peers)]
        )

    def third(h):
        total = qs[h, ex].astype(f32)
        for i, copy in enumerate(q_copies[h]):
            copy.wait_recv()
            total = total + qx[h, i].astype(f32)
        qf[h, ex] = total.astype(bf16)
        a_copies[h] = go([(qf.at[h, ex], qf.at[h, ex], {"ex": p}) for p in ex_peers])

    head(0)
    out_full = dot(r["attn"][...], branch, OUTER).astype(bf16)
    ob[0] = out_full[:, :half]
    ob[1] = out_full[:, half:]
    out_one = go([(ob.at[1 - row], ol, mate)])
    finish(0)
    for h in range(1, heads):
        head(h)
        second(h - 1)
        finish(h)
        if h == 1:
            out_one[0].wait_recv()
            both = ob[row].astype(f32) + ol[...].astype(f32)
            os_[...] = both.astype(bf16).reshape(os_.shape)
            out_two = go([(os_.at[p], ox.at[i], {"ex": p}) for i, p in enumerate(ex_peers)])
    rows = jnp.concatenate([st[h] for h in range(heads)], axis=1)
    d_xn = dot(rows, qkvw[...], INNER)
    xb, xl = r["xb"], r["xl"]
    xb[...] = d_xn.astype(bf16).reshape(xb.shape)
    x_copies = go([(xb.at[p], xl.at[i], {"col": p}) for i, p in enumerate(col_peers)])
    second(heads - 1)
    diags = [diagonals_of(r["dsc"][h].astype(f32), span) for h in range(heads)]
    diag = jnp.concatenate(diags + [jnp.zeros((8 - heads, span), f32)], axis=0)
    sa[:1, :width] = jnp.sum(d_xn * r["unit"][...], axis=0, keepdims=True)
    sa[:, width:] = dot(diag, r["rows_t"][...], precision=HIGH)
    sb = r["sb"]
    small_one = go([(sa, r["sl"], mate)])
    third(0)
    small_one[0].wait_recv()
    sb[0] = sa[...] + r["sl"][...]
    small_two = go([(sb.at[0], r["sx"].at[i], {"ex": p}) for i, p in enumerate(ex_peers)])
    third(1)
    total = os_[ex].astype(f32)
    for i, copy in enumerate(out_two):
        copy.wait_recv()
        total = total + ox[i].astype(f32)
    of_[ex] = total.astype(bf16)
    out_three = go([(of_.at[ex], of_.at[ex], {"ex": p}) for p in ex_peers])
    for h in range(2, heads):
        third(h)
    d_own = xb[col].astype(f32)
    for i, copy in enumerate(x_copies):
        copy.wait_recv()
        d_own = d_own + xl[i].astype(f32)
    unit_q, inv_q = normed(tokens[here, :])
    u1 = gain1 * d_own
    inner = jnp.mean(u1 * unit_q, axis=1, keepdims=True)
    r["input_grad"][...] = r["ds"][...] + inv_q * (u1 - unit_q * inner)
    total = sb[0]
    for i, copy in enumerate(small_two):
        copy.wait_recv()
        total = total + r["sx"][i]
    sb[1] = total
    small_three = go([(sb.at[1], r["sc"].at[i], {"col": p}) for i, p in enumerate(col_peers)])
    for h in range(heads):
        for copy in a_copies[h]:
            copy.wait_recv()
        piece = qf[h].astype(f32).reshape(tri, half)
        r["qkv_grad"][:, h * tri : (h + 1) * tri] = piece.T
    for copy in out_three:
        copy.wait_recv()
    r["out_grad"][...] = of_[...].astype(f32).reshape(r["out_grad"].shape)
    total = sb[1]
    for i, copy in enumerate(small_three):
        copy.wait_recv()
        total = total + r["sc"][i]
    r["small"][:, :width] = total[:, :width]
    r["small"][:, width:] = sb[1, :, width:]
    for copy in everything:
        copy.wait_send()


def whole_block(buckets, heads, cap, **arrays):
    n_ex, n_col = lax.axis_size("ex"), lax.axis_size("col")
    bf16, f32 = jnp.bfloat16, jnp.float32
    count, width = arrays["tokens"].shape
    quarter = count // n_col
    group, half, tri = 2 * count, width // 2, 3 * HDIM
    span = -(-(count + group - 1) // 128) * 128
    cols = arrays["expert_in"].shape[2]
    hr = arrays["out_weight"].shape[0]
    wide = width + 128
    outs = {
        "output": (quarter, width),
        "input_grad": (quarter, width),
        "qkv_grad": (half, heads * tri),
        "out_grad": (hr, half),
        "small": (8, wide),
        "g_in": (1, width, cols),
        "g_out": (1, cols, width),
    }
    narrow = {
        "tf": (group, width),
        "qkvw": (width, heads * tri),
        "outw": (hr, width),
        "p_in": (width, cols),
        "p_out": (cols, width),
        "xn": (group, width),
        "qkv": (group, heads * tri),
        "q": (heads, count, HDIM),
        "k": (heads, group, HDIM),
        "v": (heads, group, HDIM),
        "attn": (count, hr),
        "bb": (n_col, quarter, width),
        "bl": (n_col - 1, quarter, width),
        "outb": (n_ex, 2 * cap, width),
        "land": (n_col, n_ex, 2 * cap, width),
        "part": (n_col, n_ex, 2 * cap, width),
        "got": (n_col - 1, n_ex, 2 * cap, width),
        "summed": (n_ex, 2 * cap, width),
        "back": (n_ex, 2 * cap, width),
        "s_in": (width, cols),
        "s_out": (cols, width),
        "r_in": (width, cols),
        "r_out": (cols, width),
        "ba": (n_col, quarter, width),
        "dsc": (heads, count, group),
        "kvb": (heads, 2, count, 2 * HDIM),
        "kvl": (heads, count, 2 * HDIM),
        "st": (heads, count, tri),
        "tb": (heads, 2, tri, half),
        "tl": (heads, tri, half),
        "qs": (heads, n_ex, tri // n_ex, half),
        "qx": (heads, n_ex - 1, tri // n_ex, half),
        "qf": (heads, n_ex, tri // n_ex, half),
        "ob": (2, hr, half),
        "ol": (hr, half),
        "os": (n_ex, hr // n_ex, half),
        "ox": (n_ex - 1, hr // n_ex, half),
        "of": (n_ex, hr // n_ex, half),
        "xb": (n_col, quarter, width),
        "xl": (n_col - 1, quarter, width),
    }
    full = {
        "rows_t": (span, 128),
        "prob": (heads, count, group),
        "unit": (count, width),
        "ds": (quarter, width),
        "sa": (8, wide),
        "sl": (8, wide),
        "sx": (n_ex - 1, 8, wide),
        "sb": (2, 8, wide),
        "sc": (n_col - 1, 8, wide),
    }
    names = [*arrays, *outs, *narrow, *full, "send", "recv"]
    dims = (n_ex, n_col, heads, cap, buckets, count, width, quarter)
    return pl.pallas_call(
        lambda *refs: whole_kernel(dims, names, *refs),
        out_shape=tuple(jax.ShapeDtypeStruct(shape, f32) for shape in outs.values()),
        in_specs=[VMEM] * len(arrays),
        out_specs=(VMEM,) * len(outs),
        scratch_shapes=[pltpu.VMEM(shape, bf16) for shape in narrow.values()]
        + [pltpu.VMEM(shape, f32) for shape in full.values()]
        + [DMA((96,)), DMA((96,))],
        compiler_params=params(8),
    )(*arrays.values())


def expert_exchange(outbound, w_in, w_out):
    n_ex, twice, width = outbound.shape
    cap = twice // 2
    arrived = lax.all_to_all(outbound, "ex", split_axis=0, concat_axis=0, tiled=True)
    arrived = lax.all_gather(arrived, "col", axis=0, tiled=True)
    x = arrived[:, :cap].reshape(-1, width)
    g = arrived[:, cap:].reshape(-1, width)
    inner = lax.all_gather(w_in, "row", axis=1, tiled=True)
    outer = lax.all_gather(w_out, "row", axis=0, tiled=True)
    pre = jnp.dot(x, inner, preferred_element_type=jnp.float32)
    value, slope = gelu_parts(pre)
    hid = value.astype(jnp.bfloat16)
    y = jnp.dot(hid, outer, preferred_element_type=jnp.float32)
    d_hid = lax.dot_general(g, outer, INNER, preferred_element_type=jnp.float32)
    d_pre = (d_hid * slope).astype(jnp.bfloat16)
    d = lax.dot_general(d_pre, inner, INNER, preferred_element_type=jnp.float32)
    g_in = lax.dot_general(x, d_pre, OUTER, preferred_element_type=jnp.float32)
    g_out = lax.dot_general(hid, g, OUTER, preferred_element_type=jnp.float32)
    both = jnp.concatenate([y.reshape(-1, cap, width), d.reshape(-1, cap, width)], axis=1)
    both = lax.psum_scatter(both, "col", scatter_dimension=0, tiled=True).astype(jnp.bfloat16)
    back = lax.all_to_all(both, "ex", split_axis=0, concat_axis=0, tiled=True)
    g_in = lax.psum_scatter(g_in, "row", scatter_dimension=1, tiled=True)
    g_out = lax.psum_scatter(g_out, "row", scatter_dimension=0, tiled=True)
    return back, g_in, g_out


def on_device(
    tokens,
    qkv_weight,
    out_weight,
    bias_table,
    first_norm_scale,
    second_norm_scale,
    router_weight,
    expert_in,
    expert_out,
    lengths,
    routes,
    slots,
    cotangent,
):
    n_col = lax.axis_size("col")
    my_row = lax.axis_index("row")
    my_col = lax.axis_index("col")
    tokens_per_device, width = tokens.shape
    dispatch_mask = tokens_per_device // n_col
    experts = router_weight.shape[1]
    cap = max(2, (4 * dispatch_mask + 3 * experts - 1) // (3 * experts))
    heads = out_weight.shape[0] // HDIM
    buckets = bias_table.shape[0]
    scale = HDIM ** (-0.5)
    if cap % 16 == 0:
        place = (routes * cap + slots).reshape(n_col, 1, dispatch_mask)
        table = jnp.pad(bias_table.T, ((0, 8 - heads), (0, 128 - buckets)))
        output, input_grad, qkv_grad, out_grad, small, inner_grad, outer_grad = whole_block(
            buckets,
            heads,
            cap,
            tokens=tokens,
            qkv_weight=qkv_weight,
            out_weight=out_weight,
            table=table,
            gain1=first_norm_scale[None, :],
            gain2=second_norm_scale[None, :],
            router=router_weight,
            expert_in=expert_in,
            expert_out=expert_out,
            lengths=lengths,
            place=place,
            cotangent=cotangent,
        )
        return (
            output,
            input_grad,
            qkv_grad,
            out_grad,
            small[:heads, width : width + buckets].T,
            small[0, :width],
            small[1, :width],
            small[2 : 2 + experts, :width].T,
            inner_grad,
            outer_grad,
        )
    qkv_rows, out_rows, group_tokens = gather_row(qkv_weight, out_weight, tokens)
    group = group_tokens.shape[0]
    local_offset = my_row * tokens_per_device
    quarter_offset = my_col * dispatch_mask
    full_sequence = group_tokens.astype(jnp.float32)
    first_inverse_norm = lax.rsqrt(
        jnp.mean(full_sequence * full_sequence, axis=1, keepdims=True) + EPS
    )
    first_unit_input = full_sequence * first_inverse_norm
    first_normed_input = (first_unit_input * first_norm_scale).astype(jnp.bfloat16)
    qkv = jnp.dot(first_normed_input, qkv_rows, preferred_element_type=jnp.float32).astype(
        jnp.bfloat16
    )
    qkv = qkv.reshape(group, heads, 3, HDIM).transpose(2, 1, 0, 3)
    queries = lax.dynamic_slice_in_dim(qkv[0], local_offset, tokens_per_device, 1)
    keys = qkv[1]
    values = qkv[2]
    ends = jnp.cumsum(lengths[0])
    places = jnp.arange(group, dtype=jnp.int32)
    segment = jnp.sum((places[:, None] >= ends[None, :]).astype(jnp.int32), axis=1)
    own_segment = lax.dynamic_slice_in_dim(segment, local_offset, tokens_per_device, 0)
    same = own_segment[:, None] == segment[None, :]
    span = -(-(tokens_per_device + group - 1) // 128) * 128
    offsets = jnp.arange(span, dtype=jnp.int32)
    shifts = jnp.where(offsets < group, offsets, offsets - span) - local_offset
    table_rows = (
        bucket_of(shifts, buckets)[:, None] == jnp.arange(buckets, dtype=jnp.int32)[None, :]
    ).astype(jnp.float32)
    bias_lines = jnp.dot(table_rows, bias_table, precision=HIGH).T

    def scores_of(query, key, line):
        raw = jnp.einsum(
            "qd,kd->qk", query, key, preferred_element_type=jnp.float32
        ) * scale + toeplitz(line, tokens_per_device, group)
        return jnp.where(same, raw, NEG)

    def attend(item):
        query, key, value, line = item
        masked = scores_of(query, key, line)
        top = jnp.max(masked, axis=1, keepdims=True)
        expo = jnp.exp(masked - top)
        total = jnp.sum(expo, axis=1, keepdims=True)
        weights = (expo / total).astype(jnp.bfloat16)
        mixed = jnp.dot(weights, value, preferred_element_type=jnp.float32)
        return (mixed, top + jnp.log(total))

    mixed, log_total = lax.map(attend, (queries, keys, values, bias_lines))
    attn = mixed.transpose(1, 0, 2).reshape(tokens_per_device, heads * HDIM).astype(jnp.bfloat16)
    branch = scatter_sum(
        jnp.dot(attn, out_rows, preferred_element_type=jnp.float32)
        .astype(jnp.bfloat16)
        .reshape(n_col, dispatch_mask, width),
        "col",
        2,
    )
    hidden_state = (
        lax.dynamic_slice_in_dim(tokens, quarter_offset, dispatch_mask, 0).astype(jnp.float32)
        + branch
    )
    second_inverse_norm = lax.rsqrt(
        jnp.mean(hidden_state * hidden_state, axis=1, keepdims=True) + EPS
    )
    second_unit_input = hidden_state * second_inverse_norm
    second_normed_input = (second_unit_input * second_norm_scale).astype(jnp.bfloat16)
    logits = jnp.dot(second_normed_input, router_weight, preferred_element_type=jnp.float32)
    peak = jnp.max(logits, axis=1, keepdims=True)
    raised = jnp.exp(logits - peak)
    gates = raised / jnp.sum(raised, axis=1, keepdims=True)
    route_here = lax.dynamic_slice_in_dim(routes, quarter_offset, dispatch_mask, 0)
    slot_here = lax.dynamic_slice_in_dim(slots, quarter_offset, dispatch_mask, 0)
    picks = (route_here[:, None] == jnp.arange(experts, dtype=jnp.int32)[None, :]).astype(
        jnp.float32
    )
    gate = jnp.sum(gates * picks, axis=1, keepdims=True)
    upstream = lax.dynamic_slice_in_dim(cotangent, quarter_offset, dispatch_mask, 0).astype(
        jnp.float32
    )
    scaled_grad = (gate * upstream).astype(jnp.bfloat16)
    place = route_here * cap + slot_here
    put = (jnp.arange(experts * cap, dtype=jnp.int32)[:, None] == place[None, :]).astype(
        jnp.bfloat16
    )
    outbound = jnp.concatenate(
        [
            jnp.dot(put, rows, preferred_element_type=jnp.float32)
            .astype(jnp.bfloat16)
            .reshape(experts, cap, width)
            for rows in (second_normed_input, scaled_grad)
        ],
        axis=1,
    )
    back, inner_grad, outer_grad = expert_exchange(outbound, expert_in[0], expert_out[0])
    expert_back_rows, entry_back = (
        lax.dot_general(
            put, rows.reshape(experts * cap, width), OUTER, preferred_element_type=jnp.float32
        )
        for rows in (back[:, :cap], back[:, cap:])
    )
    output = hidden_state + gate * expert_back_rows
    gate_grad = jnp.sum(upstream * expert_back_rows, axis=1, keepdims=True)
    logit_grad = gates * (picks * gate_grad - gate * gate_grad)
    router_part = jnp.dot(second_normed_input.astype(jnp.float32).T, logit_grad, precision=HIGH)
    second_normed_gradient = (
        jnp.dot(logit_grad, router_weight.astype(jnp.float32).T, precision=HIGH) + entry_back
    )
    second_norm_slice = jnp.sum(second_normed_gradient * second_unit_input, axis=0)
    second_scaled_input = second_norm_scale * second_normed_gradient
    state_grad = upstream + second_inverse_norm * (
        second_scaled_input
        - second_unit_input
        * jnp.mean(second_scaled_input * second_unit_input, axis=1, keepdims=True)
    )
    xn_own = lax.dynamic_slice_in_dim(first_normed_input, local_offset, tokens_per_device, 0)
    local_unit_input = lax.dynamic_slice_in_dim(
        first_unit_input, local_offset, tokens_per_device, 0
    )
    quarter_unit_input = lax.dynamic_slice_in_dim(
        local_unit_input, quarter_offset, dispatch_mask, 0
    )
    inv_quarter = lax.dynamic_slice_in_dim(
        first_inverse_norm, local_offset + quarter_offset, dispatch_mask, 0
    )
    branch_all = gather_blocks(state_grad.astype(jnp.bfloat16), "col", 5).reshape(
        tokens_per_device, width
    )
    out_full = lax.dot_general(attn, branch_all, OUTER, preferred_element_type=jnp.float32)
    attn_grad = lax.dot_general(
        branch_all, out_rows, INNER, preferred_element_type=jnp.float32
    ).astype(jnp.bfloat16)
    attn_grad = attn_grad.reshape(tokens_per_device, heads, HDIM).transpose(1, 0, 2)

    def attend_back(item):
        query, key, value, line, level, grad = item
        masked = scores_of(query, key, line)
        prob = jnp.exp(masked - level)
        weights = prob.astype(jnp.bfloat16)
        prob_grad = jnp.einsum("qd,kd->qk", grad, value, preferred_element_type=jnp.float32)
        value_grad = jnp.einsum("qk,qd->kd", weights, grad, preferred_element_type=jnp.float32)
        score_grad = (prob * (prob_grad - jnp.sum(prob_grad * prob, axis=1, keepdims=True))).astype(
            jnp.bfloat16
        )
        query_grad = jnp.dot(score_grad, key, preferred_element_type=jnp.float32) * scale
        key_grad = (
            jnp.einsum("qk,qd->kd", score_grad, query, preferred_element_type=jnp.float32) * scale
        )
        return (
            query_grad,
            key_grad,
            value_grad,
            diagonal_sums(score_grad.astype(jnp.float32), span),
        )

    query_grads, key_grads, value_grads, diagonals = lax.map(
        attend_back, (queries, keys, values, bias_lines, log_total, attn_grad)
    )
    pairs = jnp.concatenate([key_grads, value_grads], axis=0).astype(jnp.bfloat16)
    pairs = pairs.transpose(1, 0, 2).reshape(2, tokens_per_device, 2 * heads * HDIM)
    own_pairs = scatter_sum(pairs, "row", 6).reshape(tokens_per_device, 2, heads, HDIM)
    key_own, value_own = own_pairs[:, 0], own_pairs[:, 1]
    stacked = jnp.stack(
        [
            query_grads.transpose(1, 0, 2),
            key_own.reshape(tokens_per_device, heads, HDIM),
            value_own.reshape(tokens_per_device, heads, HDIM),
        ],
        axis=2,
    )
    stacked = stacked.reshape(tokens_per_device, 3 * heads * HDIM).astype(jnp.bfloat16)
    qkv_full = lax.dot_general(xn_own, stacked, OUTER, preferred_element_type=jnp.float32)
    first_normed_slice = lax.dot_general(
        stacked, qkv_rows, INNER, preferred_element_type=jnp.float32
    )
    first_norm_slice = jnp.sum(first_normed_slice * local_unit_input, axis=0)
    table_part = jnp.dot(table_rows.T, diagonals.T, precision=HIGH)
    xn_one_grad = scatter_sum(
        first_normed_slice.astype(jnp.bfloat16).reshape(n_col, dispatch_mask, width), "col", 7
    )
    first_scaled_input = first_norm_scale * xn_one_grad
    input_grad = state_grad + inv_quarter * (
        first_scaled_input
        - quarter_unit_input
        * jnp.mean(first_scaled_input * quarter_unit_input, axis=1, keepdims=True)
    )
    half = width // lax.axis_size("row")
    qkv_sum, out_sum, table_grad = lax.psum((qkv_full, out_full, table_part), ("ex", "row"))
    norm1_grad, norm2_grad, router_grad = lax.psum(
        (first_norm_slice, second_norm_slice, router_part), ("ex", "row", "col")
    )
    qkv_grad = lax.dynamic_slice_in_dim(qkv_sum, my_row * half, half, 0)
    out_grad = lax.dynamic_slice_in_dim(out_sum, my_row * half, half, 1)
    return (
        output,
        input_grad,
        qkv_grad,
        out_grad,
        table_grad,
        norm1_grad,
        norm2_grad,
        router_grad,
        inner_grad[None],
        outer_grad[None],
    )


def solution(mesh):
    return jax.shard_map(
        on_device,
        mesh=mesh,
        in_specs=(
            P(("ex", "row"), None),
            P("row", "col"),
            P("col", "row"),
            P(None, "col"),
            P(),
            P(),
            P(),
            P("ex", None, ("row", "col")),
            P("ex", ("row", "col"), None),
            P("ex", None),
            P(("ex", "row")),
            P(("ex", "row")),
            P(("ex", "row"), None),
        ),
        out_specs=(
            P(("ex", "row", "col"), None),
            P(("ex", "row", "col"), None),
            P("row", "col"),
            P("col", "row"),
            P(None, "col"),
            P(),
            P(),
            P(),
            P("ex", None, ("row", "col")),
            P("ex", ("row", "col"), None),
        ),
        check_vma=False,
    )
```
